512 devices in a mesh: space: 64 (over z, y_hi, core), sample: 8 (over x, y_lo).
Axes of the slice: x: 4, y: 8 (y_hi: 4, y_lo: 2; y = y_hi * 2 + y_lo), z: 8, core: 2. Of those that a mesh axis runs over, the one named last changes fastest.
Arguments:
- density: float32 [64, 128, 256], P('space'), may hold values from 0.05 to 1
- fixed_mask: int32 [64, 128, 256], P('space'), may hold values 0 or 1
- load_mask: int32 [64, 128, 256], P('space'), may hold values 0 or 1
- load_fields: bfloat16 [2, 8, 64, 128, 256], P(None, None, 'space'), may hold values from -6 to 6
- angle_index: int32 [8], P('sample'), may hold values from 0 to 15
Outputs:
- displacement: float32 [8, 8, 64, 128, 256], P('sample', None, 'space')
- filtered: float32 [64, 128, 256], P('space')
The draws below stay inside these ranges and needn't reach their ends.
All inputs are finite; a program needn't handle non-finite values. No bound on the sum of `fixed_mask` or of `load_mask` on one device may be relied on, other than what follows from the above.
Results may differ from the reference program's by a relative error of at most 0.00075.
Values sent between devices are 32-bit elements; how exact they have to be, the bound alone decides.
A program may use at most 64 MiB of HBM per device.

```python
import math
import jax
import jax.numpy as jnp
from jax import lax

LOADS = 8
ITERS = 2
SWEEPS = 2
ANGLES = 16
NX = 64
NY = 128
NZ = 256
SAMPLES = 8


def with_ends(drawn, rng, smallest, top_value):
    shape = drawn.shape
    place = [jax.random.randint(jax.random.fold_in(rng, axis), (), 0, shape[axis]) for axis in range(len(shape))]
    drawn = drawn.at[tuple(place)].set(smallest)
    longest = shape.index(max(shape))
    place[longest] = (place[longest] + 1) % shape[longest]
    return drawn.at[tuple(place)].set(top_value)


def steps_of(rng, extent, cuts, low, largest):
    def one(dim, blocks):
        draws = jax.random.uniform(jax.random.fold_in(jax.random.fold_in(rng, 6), dim), (blocks,), jnp.float32, low / len(cuts), largest / len(cuts))
        return jnp.repeat(jnp.exp(draws), extent[dim] // blocks).reshape((-1,) + (1,) * (len(extent) - dim - 1))

    factor_of = one(*cuts[0])
    for cut in cuts[1:]:
        factor_of = factor_of * one(*cut)
    return factor_of


def gaussian(own_key, dims, spread, limit, shards=(), held_as=jnp.bfloat16):
    array = jax.random.normal(own_key, dims, jnp.float32) * spread
    if len(shards) > 0:
        array = steps_of(own_key, dims, shards, -0.22, 0.18) * array
    return jnp.clip(array, min=-limit, max=limit).astype(held_as)


def setup_inputs(seed: int = 0) -> dict:
    key_list = jax.random.split(jax.random.key(seed), 6)
    density = jnp.clip(0.05 + 0.95 * jax.random.uniform(key_list[0], (NX, NY, NZ), jnp.float32) ** steps_of(key_list[0], (NX, NY, NZ), ((0, 64),), -0.2, 0.2), 0.05, 1.0)
    fixed_mask = with_ends((jax.random.randint(key_list[1], (NX, NY, NZ), 0, 8) < 1).astype(jnp.int32), jax.random.fold_in(key_list[1], 1), 0, 1)
    load_mask = with_ends((jax.random.randint(key_list[2], (NX, NY, NZ), 0, 4) < 1).astype(jnp.int32), jax.random.fold_in(key_list[2], 1), 0, 1)
    load_fields = gaussian(key_list[3], (2, LOADS, NX, NY, NZ), 1.0, 6.0, ((2, 64),))
    angle_index = with_ends(jax.random.randint(key_list[4], (SAMPLES,), 0, ANGLES), jax.random.fold_in(key_list[4], 1), 0, ANGLES - 1).astype(jnp.int32)
    return {"density": density, "fixed_mask": fixed_mask, "load_mask": load_mask, "load_fields": load_fields, "angle_index": angle_index}


young_floor = 0.001
filter_weight = 2.25

def neighbours(padded):
    return [padded[..., 2:, 1:-1, 1:-1], padded[..., :-2, 1:-1, 1:-1], padded[..., 1:-1, 2:, 1:-1], padded[..., 1:-1, :-2, 1:-1], padded[..., 1:-1, 1:-1, 2:], padded[..., 1:-1, 1:-1, :-2]]

def pad_all(field):
    return jnp.pad(field, [(0, 0)] * (field.ndim - 3) + [(1, 1), (1, 1), (1, 1)])

def stiffness(modulus):
    padded = pad_all(modulus)
    centre = padded[1:-1, 1:-1, 1:-1]
    return [2.0 * centre * other / (centre + other) for other in neighbours(padded)]

def operate(field, springs, free_cell, fixed_cell):
    padded = pad_all(field)
    summed = jnp.zeros_like(field)
    for spring, other in zip(springs, neighbours(padded)):
        summed = summed + spring * (field - other)
    return free_cell * summed + fixed_cell * field

def inner_sum(left, right):
    return jnp.einsum('axyz,bxyz->ab', left, right, precision=lax.Precision.HIGHEST)

def combine(field, mixing):
    return jnp.einsum('axyz,ab->bxyz', field, mixing, precision=lax.Precision.HIGHEST)

def block_solve(gram_now, rhs):
    factor = jnp.linalg.cholesky(gram_now)
    lower_part = lax.linalg.triangular_solve(factor, rhs, left_side=True, lower=True)
    return lax.linalg.triangular_solve(factor, lower_part, left_side=True, lower=True, transpose_a=True)

def reference(density, fixed_mask, load_mask, load_fields, angle_index):
    fixed_cell = fixed_mask.astype(jnp.float32)
    free_cell = 1.0 - fixed_cell
    modulus = young_floor + (1.0 - young_floor) * density ** 3
    springs = stiffness(modulus)
    inverse_diag = 1.0 / (free_cell * sum(springs) + fixed_cell)
    load_x = load_fields[0].astype(jnp.float32)
    load_y = load_fields[1].astype(jnp.float32)
    load_cells = load_mask.astype(jnp.float32) * free_cell
    weights = [0.5 * (spring / modulus) ** 2 for spring in springs]

    def solve_sample(angle_idx):
        angle_rad = angle_idx.astype(jnp.float32) * (2.0 * math.pi / ANGLES)
        forces = load_cells * (jnp.cos(angle_rad) * load_x + jnp.sin(angle_rad) * load_y)
        solution = jnp.zeros_like(forces)
        residual = forces
        precond = inverse_diag * residual
        direction = precond
        gram_now = inner_sum(residual, precond)
        for iteration in range(ITERS):
            applied = operate(direction, springs, free_cell, fixed_cell)
            step_mix = block_solve(inner_sum(direction, applied), gram_now)
            solution = solution + combine(direction, step_mix)
            residual = residual - combine(applied, step_mix)
            if iteration + 1 < ITERS:
                precond = inverse_diag * residual
                new_gram = inner_sum(residual, precond)
                keep_mix = block_solve(gram_now, new_gram)
                direction = precond + combine(direction, keep_mix)
                gram_now = new_gram
        padded = pad_all(solution)
        energy = jnp.zeros_like(modulus)
        for weight, other in zip(weights, neighbours(padded)):
            energy = energy + weight * jnp.sum((solution - other) ** 2, axis=0)
        return (solution, energy)
    solutions, energies = lax.map(solve_sample, angle_index)
    energy_sum = jnp.sum(energies, axis=0)
    sensitivity = -3.0 * density ** 2 * (1.0 - young_floor) * energy_sum / SAMPLES
    current = sensitivity
    for sweep_no in range(SWEEPS):
        padded = pad_all(current)
        beside_all = sum(neighbours(padded))
        current = (sensitivity + filter_weight * beside_all) / (1.0 + 6.0 * filter_weight)
    return (solutions, current)
```

```python
import math

import jax
import jax.numpy as jnp
from jax import lax
from jax.experimental import pallas as pl
from jax.experimental.pallas import tpu as pltpu
from jax.sharding import PartitionSpec as P

ANGLES = 16
MESH = pl.DeviceIdType.MESH
f32 = jnp.float32
bf16 = jnp.bfloat16

young_floor = 0.001
filter_weight = 2.25

NY, NZ = 128, 256
SLAB = 16
FIELDS = 16
LOADS = 8
GROUP = 8
PLANES = 64

K_TRIG = 0
K_MOD = 7
K_F = 11
K_V = 13
K_GRAM = 15
K_X = 36
K_S = 43
K_OUT = 53
COPIES = 60

SPREAD = [(d, e) for d in (-1, 0, 1) for e in (-1, 0, 1) if (d, e) != (0, 0)] + [
    (-2, 0),
    (2, 0),
]


def harmonic(a, b):
    return 2.0 * a * b / jnp.maximum(a + b, 1e-30)


def next_row(a):
    return pltpu.roll(a, a.shape[0] - 1, 0)


def last_row(a):
    return pltpu.roll(a, 1, 0)


def next_col(a):
    return pltpu.roll(a, a.shape[1] - 1, 1)


def last_col(a):
    return pltpu.roll(a, 1, 1)


def split(a):
    high = a.astype(bf16)
    return high, (a - high.astype(f32)).astype(bf16)


def spread_row(a, k):
    return jnp.broadcast_to(a[k : k + 1, :], a.shape)


def spread_col(a, k):
    return jnp.broadcast_to(a[:, k : k + 1], a.shape)


def product(a, b):
    out = []
    for i in range(LOADS):
        row = spread_row(a[i], 0) * b[0]
        for k in range(1, LOADS):
            row = row + spread_row(a[i], k) * b[k]
        out.append(row)
    return out


def product_t(a, b):
    out = []
    for i in range(LOADS):
        row = spread_row(a[0], i) * b[0]
        for k in range(1, LOADS):
            row = row + spread_row(a[k], i) * b[k]
        out.append(row)
    return out


def plus(a, b):
    return [x + y for x, y in zip(a, b)]


def minus(a, b):
    return [x - y for x, y in zip(a, b)]


def solve(a, b):
    a, b = list(a), list(b)
    for k in range(LOADS):
        scale = 1.0 / spread_row(a[k], k)
        a[k] = a[k] * scale
        b[k] = b[k] * scale
        for i in range(LOADS):
            if i != k:
                factor = spread_row(a[i], k)
                a[i] = a[i] - factor * a[k]
                b[i] = b[i] - factor * b[k]
    return b


def kernel(
    trig_in,
    den_ref,
    fix_ref,
    mask_ref,
    load_ref,
    x_out,
    f_out,
    trig,
    mod,
    dense,
    f_own,
    f_rim,
    z_own,
    z_rim,
    coef,
    e_own,
    v_own,
    v_rim,
    gram,
    gram_in,
    x_own,
    x_send,
    q_ref,
    s_own,
    s_in,
    send_sem,
    recv_sem,
    local_sem,
):
    plane = lax.axis_index("space")
    slab = lax.axis_index("sample")
    zpos = plane // GROUP
    ypos = plane % GROUP

    def at(planes, slabs):
        return ((plane + PLANES + planes) % PLANES, (slab + GROUP + slabs) % GROUP)

    def y_mate(off):
        return (zpos * GROUP + (ypos + off) % GROUP, slab)

    def z_mate(off):
        return (((zpos + off) % GROUP) * GROUP + ypos, slab)

    def copy(src, dst, k, device):
        return pltpu.make_async_remote_copy(
            src_ref=src,
            dst_ref=dst,
            send_sem=send_sem.at[k],
            recv_sem=recv_sem.at[k],
            device_id=device,
            device_id_type=MESH,
        )

    mates = [at(0, off) for off in range(1, GROUP)]
    mates += [at(d, 0) for d in (-2, -1, 1, 2)]
    mates += [at(d, e) for d in (-1, 1) for e in (-1, 1)]
    mates += [y_mate(off) for off in range(1, GROUP)]
    mates += [z_mate(off) for off in range(1, GROUP)]
    barrier = pltpu.get_barrier_semaphore()
    for mate in mates:
        pl.semaphore_signal(barrier, inc=1, device_id=mate, device_id_type=MESH)

    before = pl.multiple_of(((slab + GROUP - 1) % GROUP) * SLAB, SLAB)
    here = pl.multiple_of(slab * SLAB, SLAB)
    after = pl.multiple_of(((slab + 1) % GROUP) * SLAB, SLAB)

    def window(ref):
        return jnp.concatenate(
            [
                ref[pl.ds(before, SLAB), :][8:],
                ref[pl.ds(here, SLAB), :],
                ref[pl.ds(after, SLAB), :][:8],
            ],
            axis=0,
        )

    row = lax.broadcasted_iota(jnp.int32, (32, NZ), 0) + (slab * SLAB - 8)
    inside = jnp.where((row >= 0) & (row < NY), 1.0, 0.0).astype(f32)
    lane = lax.broadcasted_iota(jnp.int32, (32, NZ), 1)
    not_last = jnp.where(lane < NZ - 1, 1.0, 0.0).astype(f32)
    density = window(den_ref)
    free = inside * (1.0 - window(fix_ref).astype(f32))
    loaded = free * window(mask_ref).astype(f32)
    modulus = inside * (young_floor + (1.0 - young_floor) * density * density * density)
    mod[2] = modulus
    trig[0] = trig_in[...]

    for k in range(FIELDS):
        rows = jnp.concatenate(
            [
                load_ref[k, pl.ds(before, SLAB), :].astype(f32)[12:],
                load_ref[k, pl.ds(here, SLAB), :].astype(f32),
                load_ref[k, pl.ds(after, SLAB), :].astype(f32)[:4],
            ],
            axis=0,
        )
        rows = rows * loaded[4:28]
        dense[0, 24 * k : 24 * k + 24, :] = rows[:, :128]
        dense[1, 24 * k : 24 * k + 24, :] = rows[:, 128:]
    for r in range(20):
        for h in range(2):
            f_own[r, :, 128 * h : 128 * h + 128] = dense[
                h, pl.ds(r + 2, FIELDS, stride=24), :
            ]

    pl.semaphore_wait(barrier, len(mates))

    sent = []

    def send(src, dst, k, device):
        out = copy(src, dst, k, device)
        out.start()
        sent.append(out)
        return out

    mods = [
        send(mod.at[2], mod.at[2 - d], K_MOD + n, at(d, 0))
        for n, d in enumerate((-2, -1, 1, 2))
    ]
    fs = [
        send(f_own.at[pl.ds(1, 18)], f_rim.at[0], K_F, at(-1, 0)),
        send(f_own.at[pl.ds(1, 18)], f_rim.at[1], K_F + 1, at(1, 0)),
    ]
    trigs = [
        send(trig.at[0], trig.at[off], K_TRIG + off - 1, at(0, off))
        for off in range(1, GROUP)
    ]
    for c in mods:
        c.wait_recv()

    def plane_inside(d):
        there = plane + d
        return jnp.where((there >= 0) & (there < PLANES), 1.0, 0.0).astype(f32)

    m0 = modulus
    m_up = mod[3] * plane_inside(1)
    m_up2 = mod[4] * plane_inside(2)
    m_dn = mod[1] * plane_inside(-1)
    m_dn2 = mod[0] * plane_inside(-2)
    up = harmonic(m0, m_up)
    down = harmonic(m0, m_dn)

    def flat_springs(m):
        to_next = harmonic(m, next_row(m))
        right = harmonic(m, next_col(m)) * not_last
        return to_next, last_row(to_next), right, last_col(right)

    own4 = flat_springs(m0)
    springs = (up, down) + own4
    total = up + down + own4[0] + own4[1] + own4[2] + own4[3]
    inverse = 1.0 / (free * total + (1.0 - free))

    def rim_inverse(m, beyond, between):
        a, b, c, d = flat_springs(m)
        whole = beyond + between + a + b + c + d
        return 1.0 / jnp.where(whole > 0.0, whole, 1.0)

    for n in range(6):
        coef[n] = free * springs[n]
        coef[9 + n] = springs[n]
    coef[6] = inverse
    coef[7] = rim_inverse(m_up, harmonic(m_up, m_up2), up)
    coef[8] = rim_inverse(m_dn, harmonic(m_dn, m_dn2), down)

    def along(n, w):
        return coef[n, pl.ds(w, 1), :]

    @pl.loop(0, 20)
    def _(r):
        z_own[r] = f_own[r] * along(6, r + 6)

    for c in fs:
        c.wait_recv()

    @pl.loop(0, 18)
    def _(r):
        z_rim[0, r] = f_rim[0, r] * along(7, r + 7)
        z_rim[1, r] = f_rim[1, r] * along(8, r + 7)

    @pl.loop(0, 18)
    def _(r):
        w = r + 7
        z = z_own[r + 1]
        image = (
            along(0, w) * z_rim[0, r]
            + along(1, w) * z_rim[1, r]
            + along(2, w) * z_own[r + 2]
            + along(3, w) * z_own[r]
            + along(4, w) * next_col(z)
            + along(5, w) * last_col(z)
        )
        e_own[r] = image
        v_own[r] = image * along(6, w)

    vs = [
        send(v_own.at[pl.ds(1, 16)], v_rim.at[0], K_V, at(-1, 0)),
        send(v_own.at[pl.ds(1, 16)], v_rim.at[1], K_V + 1, at(1, 0)),
    ]

    contract = (((1,), (1,)), ((), ()))

    def first_gram(c, acc):
        zh, zl = split(z_own[c + 2])
        vh, vl = split(v_own[c + 1])
        fh, fl = split(f_own[c + 2])
        eh, el = split(e_own[c + 1])
        left = jnp.concatenate([zh, vh, zl, vl], axis=0)
        right = jnp.concatenate([fh, eh, fl, el, fh, eh, fl, el], axis=0)
        return acc + lax.dot_general(left, right, contract, preferred_element_type=f32)

    acc = lax.fori_loop(0, SLAB, first_gram, jnp.zeros((64, 128), f32))
    acc = acc[:32] + acc[32:]
    acc = acc + pltpu.roll(acc, 128 - 32, 1)

    for c in vs:
        c.wait_recv()

    def second_gram(c, acc):
        w = c + 8
        v = v_own[c + 1]
        image = (
            along(0, w) * v_rim[0, c]
            + along(1, w) * v_rim[1, c]
            + along(2, w) * v_own[c + 2]
            + along(3, w) * v_own[c]
            + along(4, w) * next_col(v)
            + along(5, w) * last_col(v)
        )
        vh, vl = split(v)
        nh, nl = split(image)
        left = jnp.concatenate([vh, vl], axis=0)
        right = jnp.concatenate([nh, nl, nh, nl, nh, nl, nh, nl], axis=0)
        return acc + lax.dot_general(left, right, contract, preferred_element_type=f32)

    acc2 = lax.fori_loop(0, SLAB, second_gram, jnp.zeros((32, 128), f32))
    acc2 = acc2[:16] + acc2[16:]
    acc2 = acc2 + pltpu.roll(acc2, 128 - 16, 1)

    wide = lax.broadcasted_iota(jnp.int32, (16, 128), 1)
    packed = jnp.where(
        wide < 32,
        acc[:16],
        jnp.where(
            wide < 48,
            pltpu.roll(acc[16:], 16, 1),
            jnp.where(wide < 64, pltpu.roll(acc2, 48, 1), 0.0),
        ),
    )
    for stage, mate in enumerate((lambda off: at(0, off), y_mate, z_mate)):
        gram[stage] = packed
        arriving = [
            send(
                gram.at[stage],
                gram_in.at[stage, off - 1],
                K_GRAM + 7 * stage + off - 1,
                mate(off),
            )
            for off in range(1, GROUP)
        ]
        for n, c in enumerate(arriving):
            c.wait_recv()
            packed = packed + gram_in[stage, n]

    narrow = lax.broadcasted_iota(jnp.int32, (8, 128), 1)
    for c in trigs:
        c.wait_recv()
    cosine = jnp.zeros((8, 128), f32)
    sine = jnp.zeros((8, 128), f32)
    for off in range(GROUP):
        mine = narrow % GROUP == (slab + GROUP - off) % GROUP
        cosine = jnp.where(mine, trig[off, :8, :], cosine)
        sine = jnp.where(mine, trig[off, 8:, :], sine)
    cc, cs, ss = cosine * cosine, cosine * sine, sine * sine

    mixed = packed[8:] + pltpu.roll(packed[:8], 128 - 8, 1)

    def matrix(first):
        rows = []
        for a in range(LOADS):
            rows.append(
                cc * spread_col(packed[:8], first + a)
                + cs * spread_col(mixed, first + a)
                + ss * spread_col(packed[8:], first + 8 + a)
            )
        return rows

    g0, sm, ym, tm = matrix(0), matrix(16), matrix(32), matrix(48)
    cm = minus(g0, sm)
    e = solve(cm, sm)
    level = lax.broadcasted_iota(jnp.int32, (8, 128), 0)
    p = [e[i] + jnp.where(level == i, 1.0, 0.0).astype(f32) for i in range(LOADS)]
    g1 = minus(
        product_t(p, minus(product(ym, p), product(sm, e))),
        product_t(e, minus(product(sm, p), product(g0, e))),
    )
    q = minus(solve(g0, g1), e)
    smy = minus(sm, ym)
    curv = plus(
        product_t(q, plus(product(cm, q), product(smy, p))),
        product_t(p, plus(product(smy, q), product(minus(ym, tm), p))),
    )
    alpha = solve(curv, g1)
    on_z = plus(p, product(q, alpha))
    on_v = product(p, alpha)

    place = narrow % 32
    tiles = []
    for s in range(GROUP):
        tile = jnp.zeros((8, 128), f32)
        for a in range(LOADS):
            tile = jnp.where(
                (place < 16) & (place % 8 == a), spread_col(on_z[a], s), tile
            )
            tile = jnp.where(
                (place >= 16) & (place % 8 == a), spread_col(on_v[a], s), tile
            )
        turn = jnp.where(
            place % 16 < 8, spread_col(cosine, s), spread_col(sine, s)
        )
        tiles.append(tile * turn)
    mix = jnp.concatenate(tiles, axis=0)
    mix_high, mix_low = split(mix)
    lane64 = lax.broadcasted_iota(jnp.int32, (64, 128), 1)
    mix = jnp.where(lane64 < 64, mix_high.astype(f32), mix_low.astype(f32)).astype(bf16)

    def iterates(z, v):
        zh, zl = split(z)
        vh, vl = split(v)
        basis = jnp.concatenate([zh, vh, zl, vl, zh, vh, zl, vl], axis=0)
        return jnp.dot(mix, basis, preferred_element_type=f32)

    @pl.loop(0, 18)
    def _(r):
        x = iterates(z_own[r + 1], v_own[r])
        for h in range(2):
            x_own[h, pl.ds(pl.multiple_of(r * 64, 64), 64), :] = x[
                :, 128 * h : 128 * h + 128
            ]

    for s in range(GROUP):
        for b in range(LOADS):
            for h in range(2):
                x_send[s, b, :, 128 * h : 128 * h + 128] = x_own[
                    h, pl.ds(64 + 8 * s + b, SLAB, stride=64), :
                ]

    rows_here = pl.ds(here, SLAB)
    keep = pltpu.make_async_copy(x_send.at[slab], x_out.at[:, rows_here, :], local_sem)
    keep.start()
    xs = [
        send(
            x_send.at[(slab + off) % GROUP],
            x_out.at[:, rows_here, :],
            K_X + off - 1,
            at(0, off),
        )
        for off in range(1, GROUP)
    ]

    def squares(a, b):
        d = a - b
        return jnp.sum(d * d, axis=0, keepdims=True)

    def x_row(r):
        rows = pl.ds(pl.multiple_of(r * 64, 64), 64)
        return jnp.concatenate([x_own[0, rows, :], x_own[1, rows, :]], axis=1)

    @pl.loop(0, 17)
    def _(r):
        q_ref[2, pl.ds(r, 1), :] = squares(x_row(r), x_row(r + 1))

    @pl.loop(0, 16)
    def _(c):
        x = x_row(c + 1)
        q_ref[0, pl.ds(c, 1), :] = squares(x, iterates(z_rim[0, c + 1], v_rim[0, c]))
        q_ref[1, pl.ds(c, 1), :] = squares(x, iterates(z_rim[1, c + 1], v_rim[1, c]))
        q_ref[3, pl.ds(c, 1), :] = squares(x, next_col(x))

    core = slice(8, 24)
    softness = 1.0 / m0[core]

    def weight(n):
        ratio = coef[9 + n][core] * softness
        return 0.5 * ratio * ratio

    q_y = q_ref[2]
    q_z = q_ref[3][:16]
    energy = (
        weight(0) * q_ref[0][:16]
        + weight(1) * q_ref[1][:16]
        + weight(2) * next_row(q_y)[:16]
        + weight(3) * q_y[:16]
        + weight(4) * q_z
        + weight(5) * last_col(q_z)
    )
    dens = density[core]
    s_own[...] = -3.0 * dens * dens * (1.0 - young_floor) * energy * (1.0 / GROUP)

    ss_in = [
        send(s_own, s_in.at[n], K_S + n, at(d, b)) for n, (d, b) in enumerate(SPREAD)
    ]
    for c in ss_in:
        c.wait_recv()

    def slab_of(d, b):
        if (d, b) == (0, 0):
            return s_own[...]
        there = slab + b
        ok = jnp.where((there >= 0) & (there < GROUP), 1.0, 0.0).astype(f32)
        return s_in[SPREAD.index((-d, -b))] * (ok * plane_inside(d))

    zeros8 = jnp.zeros((8, NZ), f32)
    fields = {}
    for d in (-1, 0, 1):
        fields[d] = jnp.concatenate(
            [slab_of(d, -1)[8:], slab_of(d, 0), slab_of(d, 1)[:8]], axis=0
        )
    for d in (-2, 2):
        fields[d] = jnp.concatenate([zeros8, slab_of(d, 0), zeros8], axis=0)
    not_first = jnp.where(lane > 0, 1.0, 0.0).astype(f32)

    def smooth(source, middle, above, below):
        beside = (
            above
            + below
            + next_row(middle)
            + last_row(middle)
            + next_col(middle) * not_last
            + last_col(middle) * not_first
        )
        return (source + filter_weight * beside) * (1.0 / (1.0 + 6.0 * filter_weight))

    once = {
        d: smooth(fields[d], fields[d], fields[d + 1], fields[d - 1])
        * (inside * plane_inside(d))
        for d in (-1, 0, 1)
    }
    twice = smooth(fields[0], once[0], once[1], once[-1])
    f_out[rows_here, :] = twice[core]
    outs = [
        send(
            f_out.at[rows_here, :],
            f_out.at[rows_here, :],
            K_OUT + off - 1,
            at(0, off),
        )
        for off in range(1, GROUP)
    ]
    keep.wait()
    for c in xs + outs:
        c.wait_recv()
    for c in sent:
        c.wait_send()


def body(density, fixed_mask, load_mask, load_fields, angle_index):
    angle_rad = angle_index.astype(f32) * (2.0 * math.pi / ANGLES)
    turn = jnp.stack([jnp.cos(angle_rad), jnp.sin(angle_rad)])
    trig = jnp.broadcast_to(turn[:, :, None], (2, 8, 128)).reshape(16, 128)
    vmem = pl.BlockSpec(memory_space=pltpu.VMEM)
    x, filtered = pl.pallas_call(
        kernel,
        out_shape=(
            jax.ShapeDtypeStruct((LOADS, NY, NZ), f32),
            jax.ShapeDtypeStruct((NY, NZ), f32),
        ),
        in_specs=[vmem] * 5,
        out_specs=(pl.BlockSpec(memory_space=pl.ANY), vmem),
        scratch_shapes=[
            pltpu.VMEM((8, 16, 128), f32),
            pltpu.VMEM((5, 32, NZ), f32),
            pltpu.VMEM((2, 16 * 24, 128), f32),
            pltpu.VMEM((20, 16, NZ), f32),
            pltpu.VMEM((2, 18, 16, NZ), f32),
            pltpu.VMEM((20, 16, NZ), f32),
            pltpu.VMEM((2, 18, 16, NZ), f32),
            pltpu.VMEM((16, 32, NZ), f32),
            pltpu.VMEM((18, 16, NZ), f32),
            pltpu.VMEM((18, 16, NZ), f32),
            pltpu.VMEM((2, 16, 16, NZ), f32),
            pltpu.VMEM((4, 16, 128), f32),
            pltpu.VMEM((3, 7, 16, 128), f32),
            pltpu.VMEM((2, 18 * 64, 128), f32),
            pltpu.VMEM((8, 8, 16, NZ), f32),
            pltpu.VMEM((4, 32, NZ), f32),
            pltpu.VMEM((16, NZ), f32),
            pltpu.VMEM((10, 16, NZ), f32),
            pltpu.SemaphoreType.DMA((COPIES,)),
            pltpu.SemaphoreType.DMA((COPIES,)),
            pltpu.SemaphoreType.DMA,
        ],
        compiler_params=pltpu.CompilerParams(
            collective_id=0, has_side_effects=True, vmem_limit_bytes=40 * 2**20
        ),
    )(
        trig,
        density.reshape(NY, NZ),
        fixed_mask.reshape(NY, NZ),
        load_mask.reshape(NY, NZ),
        load_fields.reshape(FIELDS, NY, NZ),
    )
    return x.reshape(1, LOADS, 1, NY, NZ), filtered.reshape(1, NY, NZ)


def solution(mesh):
    in_specs = (
        P("space", None, None),
        P("space", None, None),
        P("space", None, None),
        P(None, None, "space", None, None),
        P("sample"),
    )
    out_specs = (P("sample", None, "space", None, None), P("space", None, None))
    return jax.shard_map(body, mesh=mesh, in_specs=in_specs, out_specs=out_specs, check_vma=False)
```

```python
import math

import jax
import jax.numpy as jnp
from jax import lax
from jax.experimental import pallas as pl
from jax.experimental.pallas import tpu as pltpu
from jax.sharding import PartitionSpec as P

ANGLES = 16
MESH = pl.DeviceIdType.MESH
f32 = jnp.float32
bf16 = jnp.bfloat16

young_floor = 0.001
filter_weight = 2.25

NY, NZ = 128, 256
SLAB = 16
FIELDS = 16
LOADS = 8
GROUP = 8
PLANES = 64

K_TRIG = 0
K_MOD = 7
K_F = 11
K_V = 15
K_GRAM = 19
K_MIXED = 44
K_S = 51
K_OUT = 61
K_SCALE = 68
COPIES = 75

SPREAD = [(d, e) for d in (-1, 0, 1) for e in (-1, 0, 1) if (d, e) != (0, 0)] + [
    (-2, 0),
    (2, 0),
]


def harmonic(a, b):
    return 2.0 * a * b / jnp.maximum(a + b, 1e-30)


def next_row(a):
    return pltpu.roll(a, a.shape[0] - 1, 0)


def last_row(a):
    return pltpu.roll(a, 1, 0)


def next_col(a):
    return pltpu.roll(a, a.shape[1] - 1, 1)


def last_col(a):
    return pltpu.roll(a, 1, 1)


def split(a):
    high = a.astype(bf16)
    return high, (a - high.astype(f32)).astype(bf16)


def spread_row(a, k):
    return jnp.broadcast_to(a[k : k + 1, :], a.shape)


def spread_col(a, k):
    return jnp.broadcast_to(a[:, k : k + 1], a.shape)


def product(a, b):
    out = []
    for i in range(LOADS):
        row = spread_row(a[i], 0) * b[0]
        for k in range(1, LOADS):
            row = row + spread_row(a[i], k) * b[k]
        out.append(row)
    return out


def product_t(a, b):
    out = []
    for i in range(LOADS):
        row = spread_row(a[0], i) * b[0]
        for k in range(1, LOADS):
            row = row + spread_row(a[k], i) * b[k]
        out.append(row)
    return out


def plus(a, b):
    return [x + y for x, y in zip(a, b)]


def minus(a, b):
    return [x - y for x, y in zip(a, b)]


def solve(a, b):
    a, b = list(a), list(b)
    for k in range(LOADS):
        scale = 1.0 / spread_row(a[k], k)
        a[k] = a[k] * scale
        b[k] = b[k] * scale
        for i in range(LOADS):
            if i != k:
                factor = spread_row(a[i], k)
                a[i] = a[i] - factor * a[k]
                b[i] = b[i] - factor * b[k]
    return b


def kernel(
    trig_in,
    den_ref,
    fix_ref,
    mask_ref,
    load_ref,
    x_out,
    f_out,
    den_in,
    fix_in,
    mask_in,
    load_in,
    load_all,
    scale_all,
    z_all,
    v_all,
    x_all,
    v_send,
    v_half,
    factors,
    trig,
    mod,
    dense,
    f_own,
    f_rim,
    z_own,
    z_rim,
    coef,
    e_own,
    v_own,
    v_rim,
    gram,
    gram_in,
    x_own,
    q_ref,
    s_own,
    s_in,
    send_sem,
    recv_sem,
    fetch_sem,
    local_sem,
):
    plane = lax.axis_index("space")
    slab = lax.axis_index("sample")
    zpos = plane // GROUP
    ypos = plane % GROUP
    other_core = (plane // 2) * 2 + (plane + 1) % 2

    def at(planes, slabs):
        return ((plane + PLANES + planes) % PLANES, (slab + GROUP + slabs) % GROUP)

    def y_mate(off):
        return (zpos * GROUP + (ypos + 2 * off) % GROUP, slab)

    def z_mate(off):
        return (((zpos + off) % GROUP) * GROUP + ypos, slab)

    def copy(src, dst, k, device):
        return pltpu.make_async_remote_copy(
            src_ref=src,
            dst_ref=dst,
            send_sem=send_sem.at[k],
            recv_sem=recv_sem.at[k],
            device_id=device,
            device_id_type=MESH,
        )

    mates = [at(d, 0) for d in (-1, 1, -2, 2)]
    mates += [at(0, off) for off in range(1, GROUP)]
    mates += [at(d, e) for d in (-1, 1) for e in (-1, 1)]
    near = [(other_core, (slab + off) % GROUP) for off in range(GROUP)]
    stages = [
        [z_mate(off) for off in range(1, GROUP)],
        [y_mate(off) for off in range(1, 4)],
        [at(0, off) for off in range(1, GROUP)] + near,
    ]
    mates += stages[0] + stages[1] + near
    barrier = pltpu.get_barrier_semaphore()
    for mate in mates:
        pl.semaphore_signal(barrier, inc=1, device_id=mate, device_id_type=MESH)

    fetches = []
    for n in range(3):
        rows = pl.ds(pl.multiple_of(((slab + GROUP - 1 + n) % GROUP) * SLAB, SLAB), SLAB)
        put = pl.ds(n * SLAB, SLAB)
        for k, (src, dst) in enumerate(
            (
                (den_ref.at[rows], den_in.at[put]),
                (fix_ref.at[rows], fix_in.at[put]),
                (mask_ref.at[rows], mask_in.at[put]),
                (load_ref.at[:, rows], load_in.at[:, put]),
            )
        ):
            fetches.append(pltpu.make_async_copy(src, dst, fetch_sem.at[4 * n + k]))
    whole = pltpu.make_async_copy(load_ref, load_all, fetch_sem.at[12])
    for c in fetches + [whole]:
        c.start()
    here = pl.multiple_of(slab * SLAB, SLAB)

    def window(ref):
        return ref[8:40, :]

    row = lax.broadcasted_iota(jnp.int32, (32, NZ), 0) + (slab * SLAB - 8)
    inside = jnp.where((row >= 0) & (row < NY), 1.0, 0.0).astype(f32)
    lane = lax.broadcasted_iota(jnp.int32, (32, NZ), 1)
    not_last = jnp.where(lane < NZ - 1, 1.0, 0.0).astype(f32)
    for c in fetches:
        c.wait()
    density = window(den_in)
    free = inside * (1.0 - window(fix_in).astype(f32))
    loaded = free * window(mask_in).astype(f32)
    modulus = inside * (young_floor + (1.0 - young_floor) * density * density * density)
    mod[2] = modulus
    trig[0] = trig_in[...]

    for k in range(FIELDS):
        rows = load_in[k].astype(f32)[8:40] * loaded
        dense[0, 32 * k : 32 * k + 32, :] = rows[:, :128]
        dense[1, 32 * k : 32 * k + 32, :] = rows[:, 128:]
    for r in range(20):
        for h in range(2):
            f_own[r, :, 128 * h : 128 * h + 128] = dense[
                h, pl.ds(r + 6, FIELDS, stride=32), :
            ]

    pl.semaphore_wait(barrier, len(mates))

    sent = []

    def send(src, dst, k, device):
        out = copy(src, dst, k, device)
        out.start()
        sent.append(out)
        return out

    mods = [
        send(mod.at[2], mod.at[2 - d], K_MOD + n, at(d, 0))
        for n, d in enumerate((-2, -1, 1, 2))
    ]
    fs = []
    for half in range(2):
        src, dst = pl.ds(1 + 9 * half, 9), pl.ds(9 * half, 9)
        for n, d in enumerate((-1, 1)):
            fs.append(
                send(f_own.at[src], f_rim.at[n, dst], K_F + 2 * half + n, at(d, 0))
            )
    trigs = [
        send(trig.at[0], trig.at[off], K_TRIG + off - 1, at(0, off))
        for off in range(1, GROUP)
    ]
    for c in mods:
        c.wait_recv()

    def plane_inside(d):
        there = plane + d
        return jnp.where((there >= 0) & (there < PLANES), 1.0, 0.0).astype(f32)

    m0 = modulus
    m_up = mod[3] * plane_inside(1)
    m_up2 = mod[4] * plane_inside(2)
    m_dn = mod[1] * plane_inside(-1)
    m_dn2 = mod[0] * plane_inside(-2)
    up = harmonic(m0, m_up)
    down = harmonic(m0, m_dn)

    def flat_springs(m):
        to_next = harmonic(m, next_row(m))
        right = harmonic(m, next_col(m)) * not_last
        return to_next, last_row(to_next), right, last_col(right)

    own4 = flat_springs(m0)
    springs = (up, down) + own4
    total = up + down + own4[0] + own4[1] + own4[2] + own4[3]
    inverse = 1.0 / (free * total + (1.0 - free))

    def rim_inverse(m, beyond, between):
        a, b, c, d = flat_springs(m)
        whole = beyond + between + a + b + c + d
        return 1.0 / jnp.where(whole > 0.0, whole, 1.0)

    for n in range(6):
        coef[n] = free * springs[n]
        coef[9 + n] = springs[n]
    coef[6] = inverse
    coef[7] = rim_inverse(m_up, harmonic(m_up, m_up2), up)
    coef[8] = rim_inverse(m_dn, harmonic(m_dn, m_dn2), down)

    rows_here = pl.ds(here, SLAB)
    scale_all[rows_here, :] = (loaded * inverse)[8:24]
    scales = [
        send(
            scale_all.at[rows_here],
            scale_all.at[rows_here],
            K_SCALE + off - 1,
            at(0, off),
        )
        for off in range(1, GROUP)
    ]

    def along(n, w):
        return coef[n, pl.ds(w, 1), :]

    @pl.loop(0, 20)
    def _(r):
        z_own[r] = f_own[r] * along(6, r + 6)

    def send_v(first, n, k):
        rows = pl.ds(first, 8)
        return send(
            v_own.at[pl.ds(first + 1, 8)], v_rim.at[n, rows], K_V + k, at(2 * n - 1, 0)
        )

    vs = []
    for half in range(2):
        for c in fs[2 * half : 2 * half + 2]:
            c.wait_recv()

        @pl.loop(9 * half, 9 * half + 9)
        def _(r):
            w = r + 7
            z = z_own[r + 1]
            z_up = f_rim[0, r] * along(7, w)
            z_down = f_rim[1, r] * along(8, w)
            z_rim[0, r] = z_up
            z_rim[1, r] = z_down
            image = (
                along(0, w) * z_up
                + along(1, w) * z_down
                + along(2, w) * z_own[r + 2]
                + along(3, w) * z_own[r]
                + along(4, w) * next_col(z)
                + along(5, w) * last_col(z)
            )
            e_own[r] = image
            v = image * along(6, w)
            v_own[r] = v
            for h in range(2):
                v_half[h, pl.ds(pl.multiple_of(r * FIELDS, FIELDS), FIELDS), :] = v[
                    :, 128 * h : 128 * h + 128
                ]

        vs.append(send_v(8 * half, 1 - half, half))
    late_vs = [send_v(8, 1, 2), send_v(0, 0, 3)]

    for c in trigs:
        c.wait_recv()
    for b in range(LOADS):
        for h in range(2):
            cols = slice(128 * h, 128 * h + 128)
            v_x = v_half[h, pl.ds(FIELDS + b, SLAB, stride=FIELDS), :]
            v_y = v_half[h, pl.ds(FIELDS + LOADS + b, SLAB, stride=FIELDS), :]
            for off in range(GROUP):
                turn = trig[(GROUP - off) % GROUP]
                mixed = turn[0:1] * v_x + turn[8:9] * v_y
                if off == 0:
                    v_all[b, rows_here, cols] = mixed
                else:
                    v_send[off, b, :, cols] = mixed

    mixed_vs = [
        send(
            v_send.at[off],
            v_all.at[:, rows_here, :],
            K_MIXED + off - 1,
            at(0, off),
        )
        for off in (2, 6, 4)
    ]
    contract = (((1,), (1,)), ((), ()))

    def first_gram(c, acc):
        w = c + 8
        v = v_own[c + 1]
        flat = (
            along(2, w) * v_own[c + 2]
            + along(3, w) * v_own[c]
            + along(4, w) * next_col(v)
            + along(5, w) * last_col(v)
        )
        zh, zl = split(z_own[c + 2])
        vh, vl = split(v)
        fh, fl = split(f_own[c + 2])
        eh, el = split(e_own[c + 1])
        nh, nl = split(flat)
        left = jnp.concatenate([zh, vh, zl, vl], axis=0)
        right = jnp.concatenate([fh, eh, fl, el, nh, nl, nh, nl], axis=0)
        return acc + lax.dot_general(left, right, contract, preferred_element_type=f32)

    acc = lax.fori_loop(0, SLAB, first_gram, jnp.zeros((64, 128), f32))
    acc = acc[:32] + acc[32:]
    flat_part = acc[16:]
    flat_part = flat_part + pltpu.roll(flat_part, 128 - 16, 1)
    acc = acc + pltpu.roll(acc, 128 - 32, 1)

    def second_gram(n, coef_n):
        def step(c, acc):
            vh, vl = split(v_own[c + 1])
            wh, wl = split(along(coef_n, c + 8) * v_rim[n, c])
            left = jnp.concatenate([vh, vl, wh, wl], axis=0)
            right = jnp.concatenate([wh, wl, vh, vl, wh, wl, vh, vl], axis=0)
            return acc + lax.dot_general(
                left, right, contract, preferred_element_type=f32
            )

        return step

    acc2 = jnp.zeros((64, 128), f32)
    vs[0].wait_recv()
    acc2 = lax.fori_loop(0, 8, second_gram(1, 1), acc2)
    vs[1].wait_recv()
    acc2 = lax.fori_loop(8, 16, second_gram(0, 0), acc2)
    acc2 = acc2[:32] + pltpu.roll(acc2[32:], 128 - 32, 1)
    acc2 = acc2[:16] + acc2[16:]
    acc2 = acc2 + pltpu.roll(acc2, 128 - 16, 1)

    wide = lax.broadcasted_iota(jnp.int32, (16, 128), 1)
    packed = jnp.where(
        wide < 32,
        acc[:16],
        jnp.where(
            wide < 48,
            pltpu.roll(acc[16:], 16, 1),
            jnp.where(
                wide < 64,
                pltpu.roll(acc2, 48, 1) + pltpu.roll(flat_part, 128 - 16, 1),
                0.0,
            ),
        ),
    )
    first = 0
    for stage, group in enumerate(stages):
        gram[stage] = packed
        arriving = [
            send(gram.at[stage], gram_in.at[first + n], K_GRAM + first + n, mate)
            for n, mate in enumerate(group)
        ]
        if stage == 0:
            whole.wait()
            for c in scales:
                c.wait_recv()

            @pl.loop(0, GROUP)
            def _(j):
                rows = pl.ds(pl.multiple_of(j * SLAB, SLAB), SLAB)
                by_x = scale_all[rows, :] * jnp.concatenate([trig[0, 0:1]] * 2, axis=1)
                by_y = scale_all[rows, :] * jnp.concatenate([trig[0, 8:9]] * 2, axis=1)
                for b in range(LOADS):
                    z_all[b, rows, :] = by_x * load_all[b, rows, :].astype(
                        f32
                    ) + by_y * load_all[LOADS + b, rows, :].astype(f32)

        if stage == 0:
            mixed_vs += [
                send(
                    v_send.at[off],
                    v_all.at[:, rows_here, :],
                    K_MIXED + off - 1,
                    at(0, off),
                )
                for off in (1, 7)
            ]
        for n, c in enumerate(arriving):
            c.wait_recv()
            packed = packed + gram_in[first + n]
        first += len(group)

    mixed_vs += [
        send(
            v_send.at[off],
            v_all.at[:, rows_here, :],
            K_MIXED + off - 1,
            at(0, off),
        )
        for off in (3, 5)
    ]
    narrow = lax.broadcasted_iota(jnp.int32, (8, 128), 1)
    cosine = jnp.zeros((8, 128), f32)
    sine = jnp.zeros((8, 128), f32)
    for off in range(GROUP):
        mine = narrow % GROUP == (slab + GROUP - off) % GROUP
        cosine = jnp.where(mine, trig[off, :8, :], cosine)
        sine = jnp.where(mine, trig[off, 8:, :], sine)
    cc, cs, ss = cosine * cosine, cosine * sine, sine * sine

    mixed = packed[8:] + pltpu.roll(packed[:8], 128 - 8, 1)

    def matrix(first):
        rows = []
        for a in range(LOADS):
            rows.append(
                cc * spread_col(packed[:8], first + a)
                + cs * spread_col(mixed, first + a)
                + ss * spread_col(packed[8:], first + 8 + a)
            )
        return rows

    g0, sm, ym, tm = matrix(0), matrix(16), matrix(32), matrix(48)
    cm = minus(g0, sm)
    e = solve(cm, sm)
    level = lax.broadcasted_iota(jnp.int32, (8, 128), 0)
    p = [e[i] + jnp.where(level == i, 1.0, 0.0).astype(f32) for i in range(LOADS)]
    g1 = minus(
        product_t(p, minus(product(ym, p), product(sm, e))),
        product_t(e, minus(product(sm, p), product(g0, e))),
    )
    q = minus(solve(g0, g1), e)
    smy = minus(sm, ym)
    curv = plus(
        product_t(q, plus(product(cm, q), product(smy, p))),
        product_t(p, plus(product(smy, q), product(minus(ym, tm), p))),
    )
    alpha = solve(curv, g1)
    on_z = plus(p, product(q, alpha))
    on_v = product(p, alpha)

    place = narrow % 32
    tiles = []
    for s in range(GROUP):
        tile = jnp.zeros((8, 128), f32)
        for a in range(LOADS):
            tile = jnp.where(
                (place < 16) & (place % 8 == a), spread_col(on_z[a], s), tile
            )
            tile = jnp.where(
                (place >= 16) & (place % 8 == a), spread_col(on_v[a], s), tile
            )
        turn = jnp.where(
            place % 16 < 8, spread_col(cosine, s), spread_col(sine, s)
        )
        tiles.append(tile * turn)
    mix = jnp.concatenate(tiles, axis=0)
    mix_high, mix_low = split(mix)
    lane64 = lax.broadcasted_iota(jnp.int32, (64, 128), 1)
    mix = jnp.where(lane64 < 64, mix_high.astype(f32), mix_low.astype(f32)).astype(bf16)

    def iterates(z, v):
        zh, zl = split(z)
        vh, vl = split(v)
        basis = jnp.concatenate([zh, vh, zl, vl, zh, vh, zl, vl], axis=0)
        return jnp.dot(mix, basis, preferred_element_type=f32)

    @pl.loop(0, 18)
    def _(r):
        x = iterates(z_own[r + 1], v_own[r])
        for h in range(2):
            x_own[h, pl.ds(pl.multiple_of(r * 64, 64), 64), :] = x[
                :, 128 * h : 128 * h + 128
            ]

    for c in late_vs:
        c.wait_recv()

    def squares(a, b):
        d = a - b
        return jnp.sum(d * d, axis=0, keepdims=True)

    def x_row(r):
        rows = pl.ds(pl.multiple_of(r * 64, 64), 64)
        return jnp.concatenate([x_own[0, rows, :], x_own[1, rows, :]], axis=1)

    @pl.loop(0, 17)
    def _(r):
        q_ref[2, pl.ds(r, 1), :] = squares(x_row(r), x_row(r + 1))

    @pl.loop(0, 16)
    def _(c):
        x = x_row(c + 1)
        q_ref[0, pl.ds(c, 1), :] = squares(x, iterates(z_rim[0, c + 1], v_rim[0, c]))
        q_ref[1, pl.ds(c, 1), :] = squares(x, iterates(z_rim[1, c + 1], v_rim[1, c]))
        q_ref[3, pl.ds(c, 1), :] = squares(x, next_col(x))

    core = slice(8, 24)
    softness = 1.0 / m0[core]

    def weight(n):
        ratio = coef[9 + n][core] * softness
        return 0.5 * ratio * ratio

    q_y = q_ref[2]
    q_z = q_ref[3][:16]
    energy = (
        weight(0) * q_ref[0][:16]
        + weight(1) * q_ref[1][:16]
        + weight(2) * next_row(q_y)[:16]
        + weight(3) * q_y[:16]
        + weight(4) * q_z
        + weight(5) * last_col(q_z)
    )
    dens = density[core]
    s_own[...] = -3.0 * dens * dens * (1.0 - young_floor) * energy * (1.0 / GROUP)

    ss_in = [
        send(s_own, s_in.at[n], K_S + n, at(d, b)) for n, (d, b) in enumerate(SPREAD)
    ]
    for a in range(LOADS):
        for part, rows in ((0, on_z), (1, on_v)):
            mine = jnp.where(narrow == slab, rows[a], 0.0)
            mine = jnp.broadcast_to(jnp.sum(mine, axis=1, keepdims=True), (8, 128))
            for b in range(LOADS):
                factors[(part * LOADS + a) * LOADS + b] = spread_row(mine, b)
    for c in mixed_vs:
        c.wait_recv()

    @pl.loop(0, NY // 8)
    def _(j):
        rows = pl.ds(pl.multiple_of(j * 8, 8), 8)
        for h in range(2):
            cols = slice(128 * h, 128 * h + 128)
            basis = [z_all[a, rows, cols] for a in range(LOADS)]
            basis += [v_all[a, rows, cols] for a in range(LOADS)]
            for b in range(LOADS):
                total = factors[b] * basis[0]
                for a in range(1, 2 * LOADS):
                    total = total + factors[a * LOADS + b] * basis[a]
                x_all[b, rows, cols] = total

    keep = pltpu.make_async_copy(x_all, x_out, local_sem)
    keep.start()
    for c in ss_in:
        c.wait_recv()

    def slab_of(d, b):
        if (d, b) == (0, 0):
            return s_own[...]
        there = slab + b
        ok = jnp.where((there >= 0) & (there < GROUP), 1.0, 0.0).astype(f32)
        return s_in[SPREAD.index((-d, -b))] * (ok * plane_inside(d))

    zeros8 = jnp.zeros((8, NZ), f32)
    fields = {}
    for d in (-1, 0, 1):
        fields[d] = jnp.concatenate(
            [slab_of(d, -1)[8:], slab_of(d, 0), slab_of(d, 1)[:8]], axis=0
        )
    for d in (-2, 2):
        fields[d] = jnp.concatenate([zeros8, slab_of(d, 0), zeros8], axis=0)
    not_first = jnp.where(lane > 0, 1.0, 0.0).astype(f32)

    def smooth(source, middle, above, below):
        beside = (
            above
            + below
            + next_row(middle)
            + last_row(middle)
            + next_col(middle) * not_last
            + last_col(middle) * not_first
        )
        return (source + filter_weight * beside) * (1.0 / (1.0 + 6.0 * filter_weight))

    once = {
        d: smooth(fields[d], fields[d], fields[d + 1], fields[d - 1])
        * (inside * plane_inside(d))
        for d in (-1, 0, 1)
    }
    twice = smooth(fields[0], once[0], once[1], once[-1])
    f_out[rows_here, :] = twice[core]
    outs = [
        send(
            f_out.at[rows_here, :],
            f_out.at[rows_here, :],
            K_OUT + off - 1,
            at(0, off),
        )
        for off in range(1, GROUP)
    ]
    keep.wait()
    for c in outs:
        c.wait_recv()
    for c in sent:
        c.wait_send()


def body(density, fixed_mask, load_mask, load_fields, angle_index):
    angle_rad = angle_index.astype(f32) * (2.0 * math.pi / ANGLES)
    turn = jnp.stack([jnp.cos(angle_rad), jnp.sin(angle_rad)])
    trig = jnp.broadcast_to(turn[:, :, None], (2, 8, 128)).reshape(16, 128)
    vmem = pl.BlockSpec(memory_space=pltpu.VMEM)
    x, filtered = pl.pallas_call(
        kernel,
        out_shape=(
            jax.ShapeDtypeStruct((LOADS, NY, NZ), f32),
            jax.ShapeDtypeStruct((NY, NZ), f32),
        ),
        in_specs=[vmem] + [pl.BlockSpec(memory_space=pltpu.HBM)] * 4,
        out_specs=(pl.BlockSpec(memory_space=pl.ANY), vmem),
        scratch_shapes=[
            pltpu.VMEM((48, NZ), f32),
            pltpu.VMEM((48, NZ), jnp.int32),
            pltpu.VMEM((48, NZ), jnp.int32),
            pltpu.VMEM((FIELDS, 48, NZ), bf16),
            pltpu.VMEM((FIELDS, NY, NZ), bf16),
            pltpu.VMEM((NY, NZ), f32),
            pltpu.VMEM((LOADS, NY, NZ), f32),
            pltpu.VMEM((LOADS, NY, NZ), f32),
            pltpu.VMEM((LOADS, NY, NZ), f32),
            pltpu.VMEM((GROUP, LOADS, SLAB, NZ), f32),
            pltpu.VMEM((2, 18 * FIELDS, 128), f32),
            pltpu.VMEM((2 * LOADS * LOADS, 8, 128), f32),
            pltpu.VMEM((8, 16, 128), f32),
            pltpu.VMEM((5, 32, NZ), f32),
            pltpu.VMEM((2, 16 * 32, 128), f32),
            pltpu.VMEM((20, 16, NZ), f32),
            pltpu.VMEM((2, 18, 16, NZ), f32),
            pltpu.VMEM((20, 16, NZ), f32),
            pltpu.VMEM((2, 18, 16, NZ), f32),
            pltpu.VMEM((16, 32, NZ), f32),
            pltpu.VMEM((18, 16, NZ), f32),
            pltpu.VMEM((18, 16, NZ), f32),
            pltpu.VMEM((2, 16, 16, NZ), f32),
            pltpu.VMEM((3, 16, 128), f32),
            pltpu.VMEM((25, 16, 128), f32),
            pltpu.VMEM((2, 18 * 64, 128), f32),
            pltpu.VMEM((4, 32, NZ), f32),
            pltpu.VMEM((16, NZ), f32),
            pltpu.VMEM((10, 16, NZ), f32),
            pltpu.SemaphoreType.DMA((COPIES,)),
            pltpu.SemaphoreType.DMA((COPIES,)),
            pltpu.SemaphoreType.DMA((13,)),
            pltpu.SemaphoreType.DMA,
        ],
        compiler_params=pltpu.CompilerParams(
            collective_id=0, has_side_effects=True, vmem_limit_bytes=64 * 2**20
        ),
    )(
        trig,
        density.reshape(NY, NZ),
        fixed_mask.reshape(NY, NZ),
        load_mask.reshape(NY, NZ),
        load_fields.reshape(FIELDS, NY, NZ),
    )
    return x.reshape(1, LOADS, 1, NY, NZ), filtered.reshape(1, NY, NZ)


def solution(mesh):
    in_specs = (
        P("space", None, None),
        P("space", None, None),
        P("space", None, None),
        P(None, None, "space", None, None),
        P("sample"),
    )
    out_specs = (P("sample", None, "space", None, None), P("space", None, None))
    return jax.shard_map(body, mesh=mesh, in_specs=in_specs, out_specs=out_specs, check_vma=False)
```

```python
import math

import jax
import jax.numpy as jnp
from jax import lax
from jax.experimental import pallas as pl
from jax.experimental.pallas import tpu as pltpu
from jax.sharding import PartitionSpec as P

ANGLES = 16
MESH = pl.DeviceIdType.MESH
f32 = jnp.float32
bf16 = jnp.bfloat16

young_floor = 0.001
filter_weight = 2.25

NY, NZ = 128, 256
SLAB = 16
FIELDS = 16
LOADS = 8
GROUP = 8
PLANES = 64

K_TRIG = 0
K_MOD = 7
K_F = 11
K_V = 15
K_GRAM = 19
K_MIXED = 44
K_S = 51
K_OUT = 61
K_SCALE = 68
COPIES = 75

SPREAD = [(-2, 0), (2, 0), (-1, -1), (1, 1), (-1, 1), (1, -1)]
SPREAD += [(-1, 0), (1, 0), (0, -1), (0, 1)]


def harmonic(a, b):
    return 2.0 * a * b / jnp.maximum(a + b, 1e-30)


def next_row(a):
    return pltpu.roll(a, a.shape[0] - 1, 0)


def last_row(a):
    return pltpu.roll(a, 1, 0)


def next_col(a):
    return pltpu.roll(a, a.shape[1] - 1, 1)


def last_col(a):
    return pltpu.roll(a, 1, 1)


def split(a):
    high = a.astype(bf16)
    return high, (a - high.astype(f32)).astype(bf16)


def spread_row(a, k):
    return jnp.broadcast_to(a[k : k + 1, :], a.shape)


def spread_col(a, k):
    return jnp.broadcast_to(a[:, k : k + 1], a.shape)


def product(a, b):
    out = []
    for i in range(LOADS):
        row = spread_row(a[i], 0) * b[0]
        for k in range(1, LOADS):
            row = row + spread_row(a[i], k) * b[k]
        out.append(row)
    return out


def product_t(a, b):
    out = []
    for i in range(LOADS):
        row = spread_row(a[0], i) * b[0]
        for k in range(1, LOADS):
            row = row + spread_row(a[k], i) * b[k]
        out.append(row)
    return out


def plus(a, b):
    return [x + y for x, y in zip(a, b)]


def minus(a, b):
    return [x - y for x, y in zip(a, b)]


def solve(a, b):
    a, b = list(a), list(b)
    for k in range(LOADS):
        scale = 1.0 / spread_row(a[k], k)
        a[k] = a[k] * scale
        b[k] = b[k] * scale
        for i in range(LOADS):
            if i != k:
                factor = spread_row(a[i], k)
                a[i] = a[i] - factor * a[k]
                b[i] = b[i] - factor * b[k]
    return b


def kernel(
    angle_ref,
    den_ref,
    fix_ref,
    mask_ref,
    load_ref,
    x_out,
    f_out,
    den_in,
    fix_in,
    mask_in,
    load_in,
    load_all,
    scale_all,
    z_all,
    v_all,
    x_all,
    v_send,
    v_half,
    factors,
    trig,
    mod,
    dense,
    f_own,
    f_rim,
    z_own,
    z_rim,
    coef,
    e_own,
    v_own,
    v_rim,
    gram,
    gram_in,
    x_own,
    q_ref,
    s_own,
    s_in,
    send_sem,
    recv_sem,
    fetch_sem,
    local_sem,
):
    plane = lax.axis_index("space")
    slab = lax.axis_index("sample")
    zpos = plane // GROUP
    ypos = plane % GROUP
    other_core = (plane // 2) * 2 + (plane + 1) % 2

    def at(planes, slabs):
        return ((plane + PLANES + planes) % PLANES, (slab + GROUP + slabs) % GROUP)

    def y_mate(off):
        return (zpos * GROUP + (ypos + 2 * off) % GROUP, slab)

    def z_mate(off):
        return (((zpos + off) % GROUP) * GROUP + ypos, slab)

    def copy(src, dst, k, device):
        return pltpu.make_async_remote_copy(
            src_ref=src,
            dst_ref=dst,
            send_sem=send_sem.at[k],
            recv_sem=recv_sem.at[k],
            device_id=device,
            device_id_type=MESH,
        )

    mates = [at(d, 0) for d in (-1, 1, -2, 2)]
    mates += [at(0, off) for off in range(1, GROUP)]
    mates += [at(d, e) for d in (-1, 1) for e in (-1, 1)]
    near = [(other_core, (slab + off) % GROUP) for off in range(GROUP)]
    stages = [
        [z_mate(off) for off in (4, 3, 5, 2, 6, 1, 7)],
        [y_mate(off) for off in (2, 1, 3)],
        near[3:6] + [at(0, off) for off in (4, 3, 5, 2, 6, 1, 7)] + near[6:] + near[:3],
    ]
    mates += stages[0] + stages[1] + near
    barrier = pltpu.get_barrier_semaphore()
    for mate in mates:
        pl.semaphore_signal(barrier, inc=1, device_id=mate, device_id_type=MESH)

    fetches = []
    for n in range(3):
        rows = pl.ds(pl.multiple_of(((slab + GROUP - 1 + n) % GROUP) * SLAB, SLAB), SLAB)
        put = pl.ds(n * SLAB, SLAB)
        for k, (src, dst) in enumerate(
            (
                (den_ref.at[rows], den_in.at[put]),
                (fix_ref.at[rows], fix_in.at[put]),
                (mask_ref.at[rows], mask_in.at[put]),
                (load_ref.at[:, rows], load_in.at[:, put]),
            )
        ):
            fetches.append(pltpu.make_async_copy(src, dst, fetch_sem.at[4 * n + k]))
    whole = pltpu.make_async_copy(load_ref, load_all, fetch_sem.at[12])
    for c in fetches + [whole]:
        c.start()
    here = pl.multiple_of(slab * SLAB, SLAB)

    def window(ref):
        return ref[8:40, :]

    row = lax.broadcasted_iota(jnp.int32, (32, NZ), 0) + (slab * SLAB - 8)
    inside = jnp.where((row >= 0) & (row < NY), 1.0, 0.0).astype(f32)
    lane = lax.broadcasted_iota(jnp.int32, (32, NZ), 1)
    not_last = jnp.where(lane < NZ - 1, 1.0, 0.0).astype(f32)
    for c in fetches:
        c.wait()
    density = window(den_in)
    free = inside * (1.0 - window(fix_in).astype(f32))
    loaded = free * window(mask_in).astype(f32)
    modulus = inside * (young_floor + (1.0 - young_floor) * density * density * density)
    mod[2] = modulus
    turned = jnp.full((8, 128), angle_ref[0], jnp.int32).astype(f32)
    turned = turned * (2.0 * math.pi / ANGLES)
    trig[0, :8, :] = jnp.cos(turned)
    trig[0, 8:, :] = jnp.sin(turned)

    for k in range(FIELDS):
        rows = load_in[k].astype(f32)[8:40] * loaded
        dense[0, 32 * k : 32 * k + 32, :] = rows[:, :128]
        dense[1, 32 * k : 32 * k + 32, :] = rows[:, 128:]
    for r in range(20):
        for h in range(2):
            f_own[r, :, 128 * h : 128 * h + 128] = dense[
                h, pl.ds(r + 6, FIELDS, stride=32), :
            ]

    pl.semaphore_wait(barrier, len(mates))

    sent = []

    def send(src, dst, k, device):
        out = copy(src, dst, k, device)
        out.start()
        sent.append(out)
        return out

    mods = [
        send(mod.at[2], mod.at[2 - d], K_MOD + n, at(d, 0))
        for n, d in enumerate((-2, -1, 1, 2))
    ]
    fs = []
    for half in range(2):
        src, dst = pl.ds(1 + 9 * half, 9), pl.ds(9 * half, 9)
        for n, d in enumerate((-1, 1)):
            fs.append(
                send(f_own.at[src], f_rim.at[n, dst], K_F + 2 * half + n, at(d, 0))
            )
    trigs = [
        send(trig.at[0], trig.at[off], K_TRIG + off - 1, at(0, off))
        for off in range(1, GROUP)
    ]
    for c in mods:
        c.wait_recv()

    def plane_inside(d):
        there = plane + d
        return jnp.where((there >= 0) & (there < PLANES), 1.0, 0.0).astype(f32)

    m0 = modulus
    m_up = mod[3] * plane_inside(1)
    m_up2 = mod[4] * plane_inside(2)
    m_dn = mod[1] * plane_inside(-1)
    m_dn2 = mod[0] * plane_inside(-2)
    up = harmonic(m0, m_up)
    down = harmonic(m0, m_dn)

    def flat_springs(m):
        to_next = harmonic(m, next_row(m))
        right = harmonic(m, next_col(m)) * not_last
        return to_next, last_row(to_next), right, last_col(right)

    own4 = flat_springs(m0)
    springs = (up, down) + own4
    total = up + down + own4[0] + own4[1] + own4[2] + own4[3]
    inverse = 1.0 / (free * total + (1.0 - free))

    def rim_inverse(m, beyond, between):
        a, b, c, d = flat_springs(m)
        whole = beyond + between + a + b + c + d
        return 1.0 / jnp.where(whole > 0.0, whole, 1.0)

    for n in range(6):
        coef[n] = free * springs[n]
        coef[9 + n] = springs[n]
    coef[6] = inverse
    coef[7] = rim_inverse(m_up, harmonic(m_up, m_up2), up)
    coef[8] = rim_inverse(m_dn, harmonic(m_dn, m_dn2), down)

    rows_here = pl.ds(here, SLAB)
    scale_all[rows_here, :] = (loaded * inverse)[8:24]
    def along(n, w):
        return coef[n, pl.ds(w, 1), :]

    @pl.loop(0, 20)
    def _(r):
        z_own[r] = f_own[r] * along(6, r + 6)

    def send_v(first, n, k):
        rows = pl.ds(first, 8)
        return send(
            v_own.at[pl.ds(first + 1, 8)], v_rim.at[n, rows], K_V + k, at(2 * n - 1, 0)
        )

    vs = []
    for half in range(2):
        for c in fs[2 * half : 2 * half + 2]:
            c.wait_recv()

        @pl.loop(9 * half, 9 * half + 9)
        def _(r):
            w = r + 7
            z = z_own[r + 1]
            z_up = f_rim[0, r] * along(7, w)
            z_down = f_rim[1, r] * along(8, w)
            z_rim[0, r] = z_up
            z_rim[1, r] = z_down
            image = (
                along(0, w) * z_up
                + along(1, w) * z_down
                + along(2, w) * z_own[r + 2]
                + along(3, w) * z_own[r]
                + along(4, w) * next_col(z)
                + along(5, w) * last_col(z)
            )
            e_own[r] = image
            v = image * along(6, w)
            v_own[r] = v
            for h in range(2):
                v_half[h, pl.ds(pl.multiple_of(r * FIELDS, FIELDS), FIELDS), :] = v[
                    :, 128 * h : 128 * h + 128
                ]

        vs.append(send_v(8 * half, 1 - half, half))
    late_vs = [send_v(8, 1, 2), send_v(0, 0, 3)]
    scales = [
        send(
            scale_all.at[rows_here],
            scale_all.at[rows_here],
            K_SCALE + off - 1,
            at(0, off),
        )
        for off in range(1, GROUP)
    ]

    for c in trigs:
        c.wait_recv()
    for b in range(LOADS):
        for h in range(2):
            cols = slice(128 * h, 128 * h + 128)
            v_x = v_half[h, pl.ds(FIELDS + b, SLAB, stride=FIELDS), :]
            v_y = v_half[h, pl.ds(FIELDS + LOADS + b, SLAB, stride=FIELDS), :]
            for off in range(GROUP):
                turn = trig[(GROUP - off) % GROUP]
                mixed = turn[0:1] * v_x + turn[8:9] * v_y
                if off == 0:
                    v_all[b, rows_here, cols] = mixed
                else:
                    v_send[off, b, :, cols] = mixed

    mixed_vs = [
        send(
            v_send.at[off],
            v_all.at[:, rows_here, :],
            K_MIXED + off - 1,
            at(0, off),
        )
        for off in (2, 6, 4)
    ]
    contract = (((1,), (1,)), ((), ()))

    def first_parts(c):
        w = c + 8
        v = v_own[c + 1]
        flat = (
            along(2, w) * v_own[c + 2]
            + along(3, w) * v_own[c]
            + along(4, w) * next_col(v)
            + along(5, w) * last_col(v)
        )
        zh, zl = split(z_own[c + 2])
        vh, vl = split(v)
        fh, fl = split(f_own[c + 2])
        eh, el = split(e_own[c + 1])
        nh, nl = split(flat)
        left = jnp.concatenate([zh, vh, zl, vl], axis=0)
        right = jnp.concatenate([fh, eh, fl, el, nh, nl, nh, nl], axis=0)
        return left, right

    def second_parts(n, coef_n):
        def parts(c):
            vh, vl = split(v_own[c + 1])
            wh, wl = split(along(coef_n, c + 8) * v_rim[n, c])
            left = jnp.concatenate([vh, vl, wh, wl], axis=0)
            right = jnp.concatenate([wh, wl, vh, vl, wh, wl, vh, vl], axis=0)
            return left, right

        return parts

    def gram_of(parts, rows):
        both = [parts(c) for c in rows]
        left = jnp.concatenate([one for one, _ in both], axis=1)
        right = jnp.concatenate([one for _, one in both], axis=1)
        return lax.dot_general(left, right, contract, preferred_element_type=f32)

    def four_rows(j, acc):
        return acc + gram_of(first_parts, [4 * j + t for t in range(4)])

    acc = lax.fori_loop(0, SLAB // 4, four_rows, jnp.zeros((64, 128), f32))
    acc = acc[:32] + acc[32:]
    flat_part = acc[16:]
    flat_part = flat_part + pltpu.roll(flat_part, 128 - 16, 1)
    acc = acc + pltpu.roll(acc, 128 - 32, 1)

    vs[0].wait_recv()
    acc2 = gram_of(second_parts(1, 1), range(8))
    vs[1].wait_recv()
    acc2 = acc2 + gram_of(second_parts(0, 0), range(8, 16))
    acc2 = acc2[:32] + pltpu.roll(acc2[32:], 128 - 32, 1)
    acc2 = acc2[:16] + acc2[16:]
    acc2 = acc2 + pltpu.roll(acc2, 128 - 16, 1)

    wide = lax.broadcasted_iota(jnp.int32, (16, 128), 1)
    packed = jnp.where(
        wide < 32,
        acc[:16],
        jnp.where(
            wide < 48,
            pltpu.roll(acc[16:], 16, 1),
            jnp.where(
                wide < 64,
                pltpu.roll(acc2, 48, 1) + pltpu.roll(flat_part, 128 - 16, 1),
                0.0,
            ),
        ),
    )
    packed = jnp.where(wide[:8] < 64, packed[:8], pltpu.roll(packed[8:], 64, 1))
    first = 0
    for stage, group in enumerate(stages):
        gram[stage] = packed
        arriving = [
            send(gram.at[stage], gram_in.at[first + n], K_GRAM + first + n, mate)
            for n, mate in enumerate(group)
        ]
        if stage == 0:
            whole.wait()
            for c in scales:
                c.wait_recv()

            @pl.loop(0, GROUP)
            def _(j):
                rows = pl.ds(pl.multiple_of(j * SLAB, SLAB), SLAB)
                by_x = scale_all[rows, :] * jnp.concatenate([trig[0, 0:1]] * 2, axis=1)
                by_y = scale_all[rows, :] * jnp.concatenate([trig[0, 8:9]] * 2, axis=1)
                for b in range(LOADS):
                    z_all[b, rows, :] = by_x * load_all[b, rows, :].astype(
                        f32
                    ) + by_y * load_all[LOADS + b, rows, :].astype(f32)

        if stage == 0:
            mixed_vs += [
                send(
                    v_send.at[off],
                    v_all.at[:, rows_here, :],
                    K_MIXED + off - 1,
                    at(0, off),
                )
                for off in (1, 7)
            ]
        for n, c in enumerate(arriving):
            c.wait_recv()
            packed = packed + gram_in[first + n]
        first += len(group)

    mixed_vs += [
        send(
            v_send.at[off],
            v_all.at[:, rows_here, :],
            K_MIXED + off - 1,
            at(0, off),
        )
        for off in (3, 5)
    ]
    packed = jnp.concatenate([packed, pltpu.roll(packed, 64, 1)], axis=0)

    narrow = lax.broadcasted_iota(jnp.int32, (8, 128), 1)
    cosine = jnp.zeros((8, 128), f32)
    sine = jnp.zeros((8, 128), f32)
    for off in range(GROUP):
        mine = narrow % GROUP == (slab + GROUP - off) % GROUP
        cosine = jnp.where(mine, trig[off, :8, :], cosine)
        sine = jnp.where(mine, trig[off, 8:, :], sine)
    cc, cs, ss = cosine * cosine, cosine * sine, sine * sine

    mixed = packed[8:] + pltpu.roll(packed[:8], 128 - 8, 1)

    def matrix(first):
        rows = []
        for a in range(LOADS):
            rows.append(
                cc * spread_col(packed[:8], first + a)
                + cs * spread_col(mixed, first + a)
                + ss * spread_col(packed[8:], first + 8 + a)
            )
        return rows

    g0, sm, ym, tm = matrix(0), matrix(16), matrix(32), matrix(48)
    cm = minus(g0, sm)
    level = lax.broadcasted_iota(jnp.int32, (8, 128), 0)
    unit = [jnp.where(level == i, 1.0, 0.0).astype(f32) for i in range(LOADS)]
    g0_inverse = solve(g0, unit)
    e = solve(cm, sm)
    p = plus(e, unit)
    g1 = minus(
        product_t(p, minus(product(ym, p), product(sm, e))),
        product_t(e, minus(product(sm, p), product(g0, e))),
    )
    q = minus(product(g0_inverse, g1), e)
    smy = minus(sm, ym)
    curv = plus(
        product_t(q, plus(product(cm, q), product(smy, p))),
        product_t(p, plus(product(smy, q), product(minus(ym, tm), p))),
    )
    alpha = solve(curv, g1)
    on_z = plus(p, product(q, alpha))
    on_v = product(p, alpha)

    place = narrow % 32
    tiles = []
    for s in range(GROUP):
        tile = jnp.zeros((8, 128), f32)
        for a in range(LOADS):
            tile = jnp.where(
                (place < 16) & (place % 8 == a), spread_col(on_z[a], s), tile
            )
            tile = jnp.where(
                (place >= 16) & (place % 8 == a), spread_col(on_v[a], s), tile
            )
        turn = jnp.where(
            place % 16 < 8, spread_col(cosine, s), spread_col(sine, s)
        )
        tiles.append(tile * turn)
    mix = jnp.concatenate(tiles, axis=0)
    mix_high, mix_low = split(mix)
    lane64 = lax.broadcasted_iota(jnp.int32, (64, 128), 1)
    mix = jnp.where(lane64 < 64, mix_high.astype(f32), mix_low.astype(f32)).astype(bf16)

    def iterates(z, v):
        zh, zl = split(z)
        vh, vl = split(v)
        basis = jnp.concatenate([zh, vh, zl, vl, zh, vh, zl, vl], axis=0)
        return jnp.dot(mix, basis, preferred_element_type=f32)

    @pl.loop(0, 6)
    def _(j):
        for t in range(3):
            r = 3 * j + t
            x = iterates(z_own[r + 1], v_own[r])
            for h in range(2):
                x_own[h, pl.ds(pl.multiple_of(r * 64, 64), 64), :] = x[
                    :, 128 * h : 128 * h + 128
                ]

    for c in late_vs:
        c.wait_recv()

    def squares(a, b):
        d = a - b
        return jnp.sum(d * d, axis=0, keepdims=True)

    def x_row(r):
        rows = pl.ds(pl.multiple_of(r * 64, 64), 64)
        return jnp.concatenate([x_own[0, rows, :], x_own[1, rows, :]], axis=1)

    q_ref[2, 0:1, :] = squares(x_row(0), x_row(1))

    @pl.loop(0, 8)
    def _(j):
        for t in range(2):
            c = 2 * j + t
            x = x_row(c + 1)
            x_up = iterates(z_rim[0, c + 1], v_rim[0, c])
            x_down = iterates(z_rim[1, c + 1], v_rim[1, c])
            q_ref[0, pl.ds(c, 1), :] = squares(x, x_up)
            q_ref[1, pl.ds(c, 1), :] = squares(x, x_down)
            q_ref[2, pl.ds(c + 1, 1), :] = squares(x, x_row(c + 2))
            q_ref[3, pl.ds(c, 1), :] = squares(x, next_col(x))

    core = slice(8, 24)
    softness = 1.0 / m0[core]

    def weight(n):
        ratio = coef[9 + n][core] * softness
        return 0.5 * ratio * ratio

    q_y = q_ref[2]
    q_z = q_ref[3][:16]
    energy = (
        weight(0) * q_ref[0][:16]
        + weight(1) * q_ref[1][:16]
        + weight(2) * next_row(q_y)[:16]
        + weight(3) * q_y[:16]
        + weight(4) * q_z
        + weight(5) * last_col(q_z)
    )
    dens = density[core]
    s_own[...] = -3.0 * dens * dens * (1.0 - young_floor) * energy * (1.0 / GROUP)

    ss_in = [
        send(s_own, s_in.at[n], K_S + n, at(d, b)) for n, (d, b) in enumerate(SPREAD)
    ]
    for a in range(LOADS):
        for part, rows in ((0, on_z), (1, on_v)):
            mine = jnp.where(narrow == slab, rows[a], 0.0)
            mine = jnp.broadcast_to(jnp.sum(mine, axis=1, keepdims=True), (8, 128))
            for b in range(LOADS):
                factors[(part * LOADS + a) * LOADS + b] = spread_row(mine, b)
    for c in mixed_vs:
        c.wait_recv()

    @pl.loop(0, NY // 8)
    def _(j):
        rows = pl.ds(pl.multiple_of(j * 8, 8), 8)
        for h in range(2):
            cols = slice(128 * h, 128 * h + 128)
            basis = [z_all[a, rows, cols] for a in range(LOADS)]
            basis += [v_all[a, rows, cols] for a in range(LOADS)]
            for b in range(LOADS):
                total = factors[b] * basis[0]
                for a in range(1, 2 * LOADS):
                    total = total + factors[a * LOADS + b] * basis[a]
                x_all[b, rows, cols] = total

    keep = pltpu.make_async_copy(x_all, x_out, local_sem)
    keep.start()
    for c in ss_in:
        c.wait_recv()

    def slab_of(d, b):
        if (d, b) == (0, 0):
            return s_own[...]
        there = slab + b
        ok = jnp.where((there >= 0) & (there < GROUP), 1.0, 0.0).astype(f32)
        return s_in[SPREAD.index((-d, -b))] * (ok * plane_inside(d))

    zeros8 = jnp.zeros((8, NZ), f32)
    fields = {}
    for d in (-1, 0, 1):
        fields[d] = jnp.concatenate(
            [slab_of(d, -1)[8:], slab_of(d, 0), slab_of(d, 1)[:8]], axis=0
        )
    for d in (-2, 2):
        fields[d] = jnp.concatenate([zeros8, slab_of(d, 0), zeros8], axis=0)
    not_first = jnp.where(lane > 0, 1.0, 0.0).astype(f32)

    def smooth(source, middle, above, below):
        beside = (
            above
            + below
            + next_row(middle)
            + last_row(middle)
            + next_col(middle) * not_last
            + last_col(middle) * not_first
        )
        return (source + filter_weight * beside) * (1.0 / (1.0 + 6.0 * filter_weight))

    once = {
        d: smooth(fields[d], fields[d], fields[d + 1], fields[d - 1])
        * (inside * plane_inside(d))
        for d in (-1, 0, 1)
    }
    twice = smooth(fields[0], once[0], once[1], once[-1])
    f_out[rows_here, :] = twice[core]
    outs = [
        send(
            f_out.at[rows_here, :],
            f_out.at[rows_here, :],
            K_OUT + off - 1,
            at(0, off),
        )
        for off in range(1, GROUP)
    ]
    keep.wait()
    for c in outs:
        c.wait_recv()
    for c in sent:
        c.wait_send()


def hand_on(x_ref, f_ref, x_out, f_out, x_part, f_part, sems_in, sems_out):
    ways = [(x_ref.at[b], x_part.at[b], x_out.at[b]) for b in range(LOADS)]
    ways.append((f_ref, f_part, f_out))
    arriving = [
        pltpu.make_async_copy(src, part, sems_in.at[n])
        for n, (src, part, _) in enumerate(ways)
    ]
    leaving = [
        pltpu.make_async_copy(part, dst, sems_out.at[n])
        for n, (_, part, dst) in enumerate(ways)
    ]
    for c in arriving:
        c.start()
    for before, c in zip(arriving, leaving):
        before.wait()
        c.start()
    for c in leaving:
        c.wait()


def body(density, fixed_mask, load_mask, load_fields, angle_index):
    vmem = pl.BlockSpec(memory_space=pltpu.VMEM)
    x, filtered = pl.pallas_call(
        kernel,
        out_shape=(
            jax.ShapeDtypeStruct((LOADS, NY, NZ), f32),
            jax.ShapeDtypeStruct((NY, NZ), f32),
        ),
        in_specs=[pl.BlockSpec(memory_space=pltpu.SMEM)] + [pl.BlockSpec(memory_space=pltpu.HBM)] * 4,
        out_specs=(pl.BlockSpec(memory_space=pl.ANY), vmem),
        scratch_shapes=[
            pltpu.VMEM((48, NZ), f32),
            pltpu.VMEM((48, NZ), jnp.int32),
            pltpu.VMEM((48, NZ), jnp.int32),
            pltpu.VMEM((FIELDS, 48, NZ), bf16),
            pltpu.VMEM((FIELDS, NY, NZ), bf16),
            pltpu.VMEM((NY, NZ), f32),
            pltpu.VMEM((LOADS, NY, NZ), f32),
            pltpu.VMEM((LOADS, NY, NZ), f32),
            pltpu.VMEM((LOADS, NY, NZ), f32),
            pltpu.VMEM((GROUP, LOADS, SLAB, NZ), f32),
            pltpu.VMEM((2, 18 * FIELDS, 128), f32),
            pltpu.VMEM((2 * LOADS * LOADS, 8, 128), f32),
            pltpu.VMEM((8, 16, 128), f32),
            pltpu.VMEM((5, 32, NZ), f32),
            pltpu.VMEM((2, 16 * 32, 128), f32),
            pltpu.VMEM((20, 16, NZ), f32),
            pltpu.VMEM((2, 18, 16, NZ), f32),
            pltpu.VMEM((20, 16, NZ), f32),
            pltpu.VMEM((2, 18, 16, NZ), f32),
            pltpu.VMEM((16, 32, NZ), f32),
            pltpu.VMEM((18, 16, NZ), f32),
            pltpu.VMEM((18, 16, NZ), f32),
            pltpu.VMEM((2, 16, 16, NZ), f32),
            pltpu.VMEM((3, 8, 128), f32),
            pltpu.VMEM((25, 8, 128), f32),
            pltpu.VMEM((2, 18 * 64, 128), f32),
            pltpu.VMEM((4, 32, NZ), f32),
            pltpu.VMEM((16, NZ), f32),
            pltpu.VMEM((10, 16, NZ), f32),
            pltpu.SemaphoreType.DMA((COPIES,)),
            pltpu.SemaphoreType.DMA((COPIES,)),
            pltpu.SemaphoreType.DMA((13,)),
            pltpu.SemaphoreType.DMA,
        ],
        compiler_params=pltpu.CompilerParams(
            collective_id=0, has_side_effects=True, vmem_limit_bytes=64 * 2**20
        ),
    )(
        angle_index,
        density.reshape(NY, NZ),
        fixed_mask.reshape(NY, NZ),
        load_mask.reshape(NY, NZ),
        load_fields.reshape(FIELDS, NY, NZ),
    )
    anywhere = pl.BlockSpec(memory_space=pl.ANY)
    x, filtered = pl.pallas_call(
        hand_on,
        out_shape=(
            jax.ShapeDtypeStruct((LOADS, NY, NZ), f32),
            jax.ShapeDtypeStruct((NY, NZ), f32),
        ),
        in_specs=[anywhere] * 2,
        out_specs=(anywhere, anywhere),
        scratch_shapes=[
            pltpu.VMEM((LOADS, NY, NZ), f32),
            pltpu.VMEM((NY, NZ), f32),
            pltpu.SemaphoreType.DMA((LOADS + 1,)),
            pltpu.SemaphoreType.DMA((LOADS + 1,)),
        ],
        compiler_params=pltpu.CompilerParams(vmem_limit_bytes=64 * 2**20),
    )(x, filtered)
    return x.reshape(1, LOADS, 1, NY, NZ), filtered.reshape(1, NY, NZ)


def solution(mesh):
    in_specs = (
        P("space", None, None),
        P("space", None, None),
        P("space", None, None),
        P(None, None, "space", None, None),
        P("sample"),
    )
    out_specs = (P("sample", None, "space", None, None), P("space", None, None))
    return jax.shard_map(body, mesh=mesh, in_specs=in_specs, out_specs=out_specs, check_vma=False)
```

```python
import math

import jax
import jax.numpy as jnp
from jax import lax
from jax.experimental import pallas as pl
from jax.experimental.pallas import tpu as pltpu
from jax.sharding import PartitionSpec as P

ANGLES = 16
MESH = pl.DeviceIdType.MESH
f32 = jnp.float32
bf16 = jnp.bfloat16

young_floor = 0.001
filter_weight = 2.25

NY, NZ = 128, 256
SLAB = 16
FIELDS = 16
LOADS = 8
GROUP = 8
PLANES = 64

K_TRIG = 0
K_MOD = 7
K_F = 11
K_V = 15
K_GRAM = 19
K_MIXED = 44
K_S = 51
K_OUT = 61
K_SCALE = 68
COPIES = 75

SPREAD = [(-2, 0), (2, 0), (-1, -1), (1, 1), (-1, 1), (1, -1)]
SPREAD += [(-1, 0), (1, 0), (0, -1), (0, 1)]


def harmonic(a, b):
    return 2.0 * a * b / jnp.maximum(a + b, 1e-30)


def next_row(a):
    return pltpu.roll(a, a.shape[0] - 1, 0)


def last_row(a):
    return pltpu.roll(a, 1, 0)


def next_col(a):
    return pltpu.roll(a, a.shape[1] - 1, 1)


def last_col(a):
    return pltpu.roll(a, 1, 1)


def split(a):
    high = a.astype(bf16)
    return high, (a - high.astype(f32)).astype(bf16)


def spread_row(a, k):
    return jnp.broadcast_to(a[k : k + 1, :], a.shape)


def spread_col(a, k):
    return jnp.broadcast_to(a[:, k : k + 1], a.shape)


def product(a, b):
    out = []
    for i in range(LOADS):
        row = spread_row(a[i], 0) * b[0]
        for k in range(1, LOADS):
            row = row + spread_row(a[i], k) * b[k]
        out.append(row)
    return out


def product_t(a, b):
    out = []
    for i in range(LOADS):
        row = spread_row(a[0], i) * b[0]
        for k in range(1, LOADS):
            row = row + spread_row(a[k], i) * b[k]
        out.append(row)
    return out


def plus(a, b):
    return [x + y for x, y in zip(a, b)]


def minus(a, b):
    return [x - y for x, y in zip(a, b)]


def solve(a, b):
    a, b = list(a), list(b)
    for k in range(LOADS):
        scale = 1.0 / spread_row(a[k], k)
        a[k] = a[k] * scale
        b[k] = b[k] * scale
        for i in range(LOADS):
            if i != k:
                factor = spread_row(a[i], k)
                a[i] = a[i] - factor * a[k]
                b[i] = b[i] - factor * b[k]
    return b


def kernel(
    angle_ref,
    den_ref,
    fix_ref,
    mask_ref,
    load_ref,
    x_out,
    f_out,
    den_in,
    fix_in,
    mask_in,
    load_in,
    load_all,
    scale_all,
    z_all,
    v_all,
    x_all,
    v_send,
    v_half,
    factors,
    trig,
    mod,
    dense,
    f_own,
    f_rim,
    z_own,
    z_rim,
    coef,
    e_own,
    v_own,
    v_rim,
    gram,
    gram_in,
    x_own,
    q_ref,
    s_own,
    s_in,
    send_sem,
    recv_sem,
    fetch_sem,
    local_sem,
):
    plane = lax.axis_index("space")
    slab = lax.axis_index("sample")
    zpos = plane // GROUP
    ypos = plane % GROUP
    other_core = (plane // 2) * 2 + (plane + 1) % 2

    def at(planes, slabs):
        return ((plane + PLANES + planes) % PLANES, (slab + GROUP + slabs) % GROUP)

    def y_mate(off):
        return (zpos * GROUP + (ypos + 2 * off) % GROUP, slab)

    def z_mate(off):
        return (((zpos + off) % GROUP) * GROUP + ypos, slab)

    def copy(src, dst, k, device):
        return pltpu.make_async_remote_copy(
            src_ref=src,
            dst_ref=dst,
            send_sem=send_sem.at[k],
            recv_sem=recv_sem.at[k],
            device_id=device,
            device_id_type=MESH,
        )

    mates = [at(d, 0) for d in (-1, 1, -2, 2)]
    mates += [at(0, off) for off in range(1, GROUP)]
    mates += [at(d, e) for d in (-1, 1) for e in (-1, 1)]
    near = [(other_core, (slab + off) % GROUP) for off in range(GROUP)]
    stages = [
        [z_mate(off) for off in (4, 3, 5, 2, 6, 1, 7)],
        [y_mate(off) for off in (2, 1, 3)],
        near[3:6] + [at(0, off) for off in (4, 3, 5, 2, 6, 1, 7)] + near[6:] + near[:3],
    ]
    mates += stages[0] + stages[1] + near
    barrier = pltpu.get_barrier_semaphore()
    for mate in mates:
        pl.semaphore_signal(barrier, inc=1, device_id=mate, device_id_type=MESH)

    fetches = []
    for n in range(3):
        rows = pl.ds(pl.multiple_of(((slab + GROUP - 1 + n) % GROUP) * SLAB, SLAB), SLAB)
        put = pl.ds(n * SLAB, SLAB)
        for k, (src, dst) in enumerate(
            (
                (den_ref.at[rows], den_in.at[put]),
                (fix_ref.at[rows], fix_in.at[put]),
                (mask_ref.at[rows], mask_in.at[put]),
                (load_ref.at[:, rows], load_in.at[:, put]),
            )
        ):
            fetches.append(pltpu.make_async_copy(src, dst, fetch_sem.at[4 * n + k]))
    whole = pltpu.make_async_copy(load_ref, load_all, fetch_sem.at[12])
    for c in fetches + [whole]:
        c.start()
    here = pl.multiple_of(slab * SLAB, SLAB)

    def window(ref):
        return ref[8:40, :]

    row = lax.broadcasted_iota(jnp.int32, (32, NZ), 0) + (slab * SLAB - 8)
    inside = jnp.where((row >= 0) & (row < NY), 1.0, 0.0).astype(f32)
    lane = lax.broadcasted_iota(jnp.int32, (32, NZ), 1)
    not_last = jnp.where(lane < NZ - 1, 1.0, 0.0).astype(f32)
    for c in fetches:
        c.wait()
    density = window(den_in)
    free = inside * (1.0 - window(fix_in).astype(f32))
    loaded = free * window(mask_in).astype(f32)
    modulus = inside * (young_floor + (1.0 - young_floor) * density * density * density)
    mod[2] = modulus
    turned = jnp.full((8, 128), angle_ref[0], jnp.int32).astype(f32)
    turned = turned * (2.0 * math.pi / ANGLES)
    trig[0, :8, :] = jnp.cos(turned)
    trig[0, 8:, :] = jnp.sin(turned)

    for k in range(FIELDS):
        rows = load_in[k].astype(f32)[8:40] * loaded
        dense[0, 32 * k : 32 * k + 32, :] = rows[:, :128]
        dense[1, 32 * k : 32 * k + 32, :] = rows[:, 128:]
    for r in range(20):
        for h in range(2):
            f_own[r, :, 128 * h : 128 * h + 128] = dense[
                h, pl.ds(r + 6, FIELDS, stride=32), :
            ]

    pl.semaphore_wait(barrier, len(mates))

    sent = []

    def send(src, dst, k, device):
        out = copy(src, dst, k, device)
        out.start()
        sent.append(out)
        return out

    mods = [
        send(mod.at[2], mod.at[2 - d], K_MOD + n, at(d, 0))
        for n, d in enumerate((-2, -1, 1, 2))
    ]
    fs = []
    for half in range(2):
        src, dst = pl.ds(1 + 9 * half, 9), pl.ds(9 * half, 9)
        for n, d in enumerate((-1, 1)):
            fs.append(
                send(f_own.at[src], f_rim.at[n, dst], K_F + 2 * half + n, at(d, 0))
            )
    trigs = [
        send(trig.at[0], trig.at[off], K_TRIG + off - 1, at(0, off))
        for off in range(1, GROUP)
    ]
    for c in mods:
        c.wait_recv()

    def plane_inside(d):
        there = plane + d
        return jnp.where((there >= 0) & (there < PLANES), 1.0, 0.0).astype(f32)

    m0 = modulus
    m_up = mod[3] * plane_inside(1)
    m_up2 = mod[4] * plane_inside(2)
    m_dn = mod[1] * plane_inside(-1)
    m_dn2 = mod[0] * plane_inside(-2)
    up = harmonic(m0, m_up)
    down = harmonic(m0, m_dn)

    def flat_springs(m):
        to_next = harmonic(m, next_row(m))
        right = harmonic(m, next_col(m)) * not_last
        return to_next, last_row(to_next), right, last_col(right)

    own4 = flat_springs(m0)
    springs = (up, down) + own4
    total = up + down + own4[0] + own4[1] + own4[2] + own4[3]
    inverse = 1.0 / (free * total + (1.0 - free))

    def rim_inverse(m, beyond, between):
        a, b, c, d = flat_springs(m)
        whole = beyond + between + a + b + c + d
        return 1.0 / jnp.where(whole > 0.0, whole, 1.0)

    for n in range(6):
        coef[n] = free * springs[n]
        coef[9 + n] = springs[n]
    coef[6] = inverse
    coef[7] = rim_inverse(m_up, harmonic(m_up, m_up2), up)
    coef[8] = rim_inverse(m_dn, harmonic(m_dn, m_dn2), down)

    rows_here = pl.ds(here, SLAB)
    scale_all[rows_here, :] = (loaded * inverse)[8:24]
    def along(n, w):
        return coef[n, pl.ds(w, 1), :]

    @pl.loop(0, 20)
    def _(r):
        z_own[r] = f_own[r] * along(6, r + 6)

    def send_v(first, n, k):
        rows = pl.ds(first, 8)
        return send(
            v_own.at[pl.ds(first + 1, 8)], v_rim.at[n, rows], K_V + k, at(2 * n - 1, 0)
        )

    vs = []
    for half in range(2):
        for c in fs[2 * half : 2 * half + 2]:
            c.wait_recv()

        @pl.loop(9 * half, 9 * half + 9)
        def _(r):
            w = r + 7
            z = z_own[r + 1]
            z_up = f_rim[0, r] * along(7, w)
            z_down = f_rim[1, r] * along(8, w)
            z_rim[0, r] = z_up
            z_rim[1, r] = z_down
            image = (
                along(0, w) * z_up
                + along(1, w) * z_down
                + along(2, w) * z_own[r + 2]
                + along(3, w) * z_own[r]
                + along(4, w) * next_col(z)
                + along(5, w) * last_col(z)
            )
            e_own[r] = image
            v = image * along(6, w)
            v_own[r] = v
            for h in range(2):
                v_half[h, pl.ds(pl.multiple_of(r * FIELDS, FIELDS), FIELDS), :] = v[
                    :, 128 * h : 128 * h + 128
                ]

        vs.append(send_v(8 * half, 1 - half, half))
    late_vs = [send_v(8, 1, 2), send_v(0, 0, 3)]
    scales = [
        send(
            scale_all.at[rows_here],
            scale_all.at[rows_here],
            K_SCALE + off - 1,
            at(0, off),
        )
        for off in range(1, GROUP)
    ]

    for c in trigs:
        c.wait_recv()
    for b in range(LOADS):
        for h in range(2):
            cols = slice(128 * h, 128 * h + 128)
            v_x = v_half[h, pl.ds(FIELDS + b, SLAB, stride=FIELDS), :]
            v_y = v_half[h, pl.ds(FIELDS + LOADS + b, SLAB, stride=FIELDS), :]
            for off in range(GROUP):
                turn = trig[(GROUP - off) % GROUP]
                mixed = turn[0:1] * v_x + turn[8:9] * v_y
                if off == 0:
                    v_all[b, rows_here, cols] = mixed
                else:
                    v_send[off, b, :, cols] = mixed

    mixed_vs = [
        send(
            v_send.at[off],
            v_all.at[:, rows_here, :],
            K_MIXED + off - 1,
            at(0, off),
        )
        for off in (2, 6, 4)
    ]
    contract = (((1,), (1,)), ((), ()))

    def first_parts(c):
        w = c + 8
        v = v_own[c + 1]
        flat = (
            along(2, w) * v_own[c + 2]
            + along(3, w) * v_own[c]
            + along(4, w) * next_col(v)
            + along(5, w) * last_col(v)
        )
        zh, zl = split(z_own[c + 2])
        vh, vl = split(v)
        fh, fl = split(f_own[c + 2])
        eh, el = split(e_own[c + 1])
        nh, nl = split(flat)
        left = jnp.concatenate([zh, vh, zl, vl], axis=0)
        right = jnp.concatenate([fh, eh, fl, el, nh, nl, nh, nl], axis=0)
        return left, right

    def second_parts(n, coef_n):
        def parts(c):
            vh, vl = split(v_own[c + 1])
            wh, wl = split(along(coef_n, c + 8) * v_rim[n, c])
            left = jnp.concatenate([vh, vl, wh, wl], axis=0)
            right = jnp.concatenate([wh, wl, vh, vl, wh, wl, vh, vl], axis=0)
            return left, right

        return parts

    def gram_of(parts, rows):
        both = [parts(c) for c in rows]
        left = jnp.concatenate([one for one, _ in both], axis=1)
        right = jnp.concatenate([one for _, one in both], axis=1)
        return lax.dot_general(left, right, contract, preferred_element_type=f32)

    def four_rows(j, acc):
        return acc + gram_of(first_parts, [4 * j + t for t in range(4)])

    acc = lax.fori_loop(0, SLAB // 4, four_rows, jnp.zeros((64, 128), f32))
    acc = acc[:32] + acc[32:]
    flat_part = acc[16:]
    flat_part = flat_part + pltpu.roll(flat_part, 128 - 16, 1)
    acc = acc + pltpu.roll(acc, 128 - 32, 1)

    vs[0].wait_recv()
    acc2 = gram_of(second_parts(1, 1), range(8))
    vs[1].wait_recv()
    acc2 = acc2 + gram_of(second_parts(0, 0), range(8, 16))
    acc2 = acc2[:32] + pltpu.roll(acc2[32:], 128 - 32, 1)
    acc2 = acc2[:16] + acc2[16:]
    acc2 = acc2 + pltpu.roll(acc2, 128 - 16, 1)

    wide = lax.broadcasted_iota(jnp.int32, (16, 128), 1)
    packed = jnp.where(
        wide < 32,
        acc[:16],
        jnp.where(
            wide < 48,
            pltpu.roll(acc[16:], 16, 1),
            jnp.where(
                wide < 64,
                pltpu.roll(acc2, 48, 1) + pltpu.roll(flat_part, 128 - 16, 1),
                0.0,
            ),
        ),
    )
    packed = jnp.where(wide[:8] < 64, packed[:8], pltpu.roll(packed[8:], 64, 1))
    first = 0
    for stage, group in enumerate(stages):
        gram[stage] = packed
        arriving = [
            send(gram.at[stage], gram_in.at[first + n], K_GRAM + first + n, mate)
            for n, mate in enumerate(group)
        ]
        if stage == 0:
            whole.wait()
            for c in scales:
                c.wait_recv()

            @pl.loop(0, GROUP)
            def _(j):
                rows = pl.ds(pl.multiple_of(j * SLAB, SLAB), SLAB)
                by_x = scale_all[rows, :] * jnp.concatenate([trig[0, 0:1]] * 2, axis=1)
                by_y = scale_all[rows, :] * jnp.concatenate([trig[0, 8:9]] * 2, axis=1)
                for b in range(LOADS):
                    z_all[b, rows, :] = by_x * load_all[b, rows, :].astype(
                        f32
                    ) + by_y * load_all[LOADS + b, rows, :].astype(f32)

        if stage == 0:
            mixed_vs += [
                send(
                    v_send.at[off],
                    v_all.at[:, rows_here, :],
                    K_MIXED + off - 1,
                    at(0, off),
                )
                for off in (1, 7)
            ]
        if stage == 1:
            mixed_vs += [
                send(
                    v_send.at[off],
                    v_all.at[:, rows_here, :],
                    K_MIXED + off - 1,
                    at(0, off),
                )
                for off in (3,)
            ]
        if stage == 2:
            mixed_vs += [
                send(
                    v_send.at[off],
                    v_all.at[:, rows_here, :],
                    K_MIXED + off - 1,
                    at(0, off),
                )
                for off in (5,)
            ]
        for n, c in enumerate(arriving):
            c.wait_recv()
            packed = packed + gram_in[first + n]
        first += len(group)

    packed = jnp.concatenate([packed, pltpu.roll(packed, 64, 1)], axis=0)

    narrow = lax.broadcasted_iota(jnp.int32, (8, 128), 1)
    cosine = jnp.zeros((8, 128), f32)
    sine = jnp.zeros((8, 128), f32)
    for off in range(GROUP):
        mine = narrow % GROUP == (slab + GROUP - off) % GROUP
        cosine = jnp.where(mine, trig[off, :8, :], cosine)
        sine = jnp.where(mine, trig[off, 8:, :], sine)
    cc, cs, ss = cosine * cosine, cosine * sine, sine * sine

    mixed = packed[8:] + pltpu.roll(packed[:8], 128 - 8, 1)

    def matrix(first):
        rows = []
        for a in range(LOADS):
            rows.append(
                cc * spread_col(packed[:8], first + a)
                + cs * spread_col(mixed, first + a)
                + ss * spread_col(packed[8:], first + 8 + a)
            )
        return rows

    g0, sm, ym, tm = matrix(0), matrix(16), matrix(32), matrix(48)
    cm = minus(g0, sm)
    level = lax.broadcasted_iota(jnp.int32, (8, 128), 0)
    unit = [jnp.where(level == i, 1.0, 0.0).astype(f32) for i in range(LOADS)]
    g0_inverse = solve(g0, unit)
    e = solve(cm, sm)
    p = plus(e, unit)
    g1 = minus(
        product_t(p, minus(product(ym, p), product(sm, e))),
        product_t(e, minus(product(sm, p), product(g0, e))),
    )
    q = minus(product(g0_inverse, g1), e)
    smy = minus(sm, ym)
    curv = plus(
        product_t(q, plus(product(cm, q), product(smy, p))),
        product_t(p, plus(product(smy, q), product(minus(ym, tm), p))),
    )
    alpha = solve(curv, g1)
    on_z = plus(p, product(q, alpha))
    on_v = product(p, alpha)

    place = narrow % 32
    tiles = []
    for s in range(GROUP):
        tile = jnp.zeros((8, 128), f32)
        for a in range(LOADS):
            tile = jnp.where(
                (place < 16) & (place % 8 == a), spread_col(on_z[a], s), tile
            )
            tile = jnp.where(
                (place >= 16) & (place % 8 == a), spread_col(on_v[a], s), tile
            )
        turn = jnp.where(
            place % 16 < 8, spread_col(cosine, s), spread_col(sine, s)
        )
        tiles.append(tile * turn)
    mix = jnp.concatenate(tiles, axis=0)
    mix_high, mix_low = split(mix)
    lane64 = lax.broadcasted_iota(jnp.int32, (64, 128), 1)
    mix = jnp.where(lane64 < 64, mix_high.astype(f32), mix_low.astype(f32)).astype(bf16)

    def iterates(z, v):
        zh, zl = split(z)
        vh, vl = split(v)
        basis = jnp.concatenate([zh, vh, zl, vl, zh, vh, zl, vl], axis=0)
        return jnp.dot(mix, basis, preferred_element_type=f32)

    @pl.loop(0, 6)
    def _(j):
        for t in range(3):
            r = 3 * j + t
            x = iterates(z_own[r + 1], v_own[r])
            for h in range(2):
                x_own[h, pl.ds(pl.multiple_of(r * 64, 64), 64), :] = x[
                    :, 128 * h : 128 * h + 128
                ]

    for c in late_vs:
        c.wait_recv()

    def squares(a, b):
        d = a - b
        return jnp.sum(d * d, axis=0, keepdims=True)

    def x_row(r):
        rows = pl.ds(pl.multiple_of(r * 64, 64), 64)
        return jnp.concatenate([x_own[0, rows, :], x_own[1, rows, :]], axis=1)

    q_ref[2, 0:1, :] = squares(x_row(0), x_row(1))

    @pl.loop(0, 8)
    def _(j):
        for t in range(2):
            c = 2 * j + t
            x = x_row(c + 1)
            x_up = iterates(z_rim[0, c + 1], v_rim[0, c])
            x_down = iterates(z_rim[1, c + 1], v_rim[1, c])
            q_ref[0, pl.ds(c, 1), :] = squares(x, x_up)
            q_ref[1, pl.ds(c, 1), :] = squares(x, x_down)
            q_ref[2, pl.ds(c + 1, 1), :] = squares(x, x_row(c + 2))
            q_ref[3, pl.ds(c, 1), :] = squares(x, next_col(x))

    core = slice(8, 24)
    softness = 1.0 / m0[core]

    def weight(n):
        ratio = coef[9 + n][core] * softness
        return 0.5 * ratio * ratio

    q_y = q_ref[2]
    q_z = q_ref[3][:16]
    energy = (
        weight(0) * q_ref[0][:16]
        + weight(1) * q_ref[1][:16]
        + weight(2) * next_row(q_y)[:16]
        + weight(3) * q_y[:16]
        + weight(4) * q_z
        + weight(5) * last_col(q_z)
    )
    dens = density[core]
    s_own[...] = -3.0 * dens * dens * (1.0 - young_floor) * energy * (1.0 / GROUP)

    ss_in = [
        send(s_own, s_in.at[n], K_S + n, at(d, b)) for n, (d, b) in enumerate(SPREAD)
    ]
    for a in range(LOADS):
        for part, rows in ((0, on_z), (1, on_v)):
            mine = jnp.where(narrow == slab, rows[a], 0.0)
            mine = jnp.broadcast_to(jnp.sum(mine, axis=1, keepdims=True), (8, 128))
            for b in range(LOADS):
                factors[(part * LOADS + a) * LOADS + b] = spread_row(mine, b)
    for c in ss_in:
        c.wait_recv()

    def slab_of(d, b):
        if (d, b) == (0, 0):
            return s_own[...]
        there = slab + b
        ok = jnp.where((there >= 0) & (there < GROUP), 1.0, 0.0).astype(f32)
        return s_in[SPREAD.index((-d, -b))] * (ok * plane_inside(d))

    zeros8 = jnp.zeros((8, NZ), f32)
    fields = {}
    for d in (-1, 0, 1):
        fields[d] = jnp.concatenate(
            [slab_of(d, -1)[8:], slab_of(d, 0), slab_of(d, 1)[:8]], axis=0
        )
    for d in (-2, 2):
        fields[d] = jnp.concatenate([zeros8, slab_of(d, 0), zeros8], axis=0)
    not_first = jnp.where(lane > 0, 1.0, 0.0).astype(f32)

    def smooth(source, middle, above, below):
        beside = (
            above
            + below
            + next_row(middle)
            + last_row(middle)
            + next_col(middle) * not_last
            + last_col(middle) * not_first
        )
        return (source + filter_weight * beside) * (1.0 / (1.0 + 6.0 * filter_weight))

    once = {
        d: smooth(fields[d], fields[d], fields[d + 1], fields[d - 1])
        * (inside * plane_inside(d))
        for d in (-1, 0, 1)
    }
    twice = smooth(fields[0], once[0], once[1], once[-1])
    f_out[rows_here, :] = twice[core]
    outs = [
        send(
            f_out.at[rows_here, :],
            f_out.at[rows_here, :],
            K_OUT + off - 1,
            at(0, off),
        )
        for off in range(1, GROUP)
    ]
    for c in mixed_vs:
        c.wait_recv()

    @pl.loop(0, NY // 8)
    def _(j):
        rows = pl.ds(pl.multiple_of(j * 8, 8), 8)
        for h in range(2):
            cols = slice(128 * h, 128 * h + 128)
            basis = [z_all[a, rows, cols] for a in range(LOADS)]
            basis += [v_all[a, rows, cols] for a in range(LOADS)]
            for b in range(LOADS):
                total = factors[b] * basis[0]
                for a in range(1, 2 * LOADS):
                    total = total + factors[a * LOADS + b] * basis[a]
                x_all[b, rows, cols] = total

    keep = pltpu.make_async_copy(x_all, x_out, local_sem)
    keep.start()
    keep.wait()
    for c in outs:
        c.wait_recv()
    for c in sent:
        c.wait_send()


def hand_on(x_ref, f_ref, x_out, f_out, x_part, f_part, sems_in, sems_out):
    ways = [(x_ref.at[b], x_part.at[b], x_out.at[b]) for b in range(LOADS)]
    ways.append((f_ref, f_part, f_out))
    arriving = [
        pltpu.make_async_copy(src, part, sems_in.at[n])
        for n, (src, part, _) in enumerate(ways)
    ]
    leaving = [
        pltpu.make_async_copy(part, dst, sems_out.at[n])
        for n, (_, part, dst) in enumerate(ways)
    ]
    for c in arriving:
        c.start()
    for before, c in zip(arriving, leaving):
        before.wait()
        c.start()
    for c in leaving:
        c.wait()


def body(density, fixed_mask, load_mask, load_fields, angle_index):
    vmem = pl.BlockSpec(memory_space=pltpu.VMEM)
    x, filtered = pl.pallas_call(
        kernel,
        out_shape=(
            jax.ShapeDtypeStruct((LOADS, NY, NZ), f32),
            jax.ShapeDtypeStruct((NY, NZ), f32),
        ),
        in_specs=[pl.BlockSpec(memory_space=pltpu.SMEM)] + [pl.BlockSpec(memory_space=pltpu.HBM)] * 4,
        out_specs=(pl.BlockSpec(memory_space=pl.ANY), vmem),
        scratch_shapes=[
            pltpu.VMEM((48, NZ), f32),
            pltpu.VMEM((48, NZ), jnp.int32),
            pltpu.VMEM((48, NZ), jnp.int32),
            pltpu.VMEM((FIELDS, 48, NZ), bf16),
            pltpu.VMEM((FIELDS, NY, NZ), bf16),
            pltpu.VMEM((NY, NZ), f32),
            pltpu.VMEM((LOADS, NY, NZ), f32),
            pltpu.VMEM((LOADS, NY, NZ), f32),
            pltpu.VMEM((LOADS, NY, NZ), f32),
            pltpu.VMEM((GROUP, LOADS, SLAB, NZ), f32),
            pltpu.VMEM((2, 18 * FIELDS, 128), f32),
            pltpu.VMEM((2 * LOADS * LOADS, 8, 128), f32),
            pltpu.VMEM((8, 16, 128), f32),
            pltpu.VMEM((5, 32, NZ), f32),
            pltpu.VMEM((2, 16 * 32, 128), f32),
            pltpu.VMEM((20, 16, NZ), f32),
            pltpu.VMEM((2, 18, 16, NZ), f32),
            pltpu.VMEM((20, 16, NZ), f32),
            pltpu.VMEM((2, 18, 16, NZ), f32),
            pltpu.VMEM((16, 32, NZ), f32),
            pltpu.VMEM((18, 16, NZ), f32),
            pltpu.VMEM((18, 16, NZ), f32),
            pltpu.VMEM((2, 16, 16, NZ), f32),
            pltpu.VMEM((3, 8, 128), f32),
            pltpu.VMEM((25, 8, 128), f32),
            pltpu.VMEM((2, 18 * 64, 128), f32),
            pltpu.VMEM((4, 32, NZ), f32),
            pltpu.VMEM((16, NZ), f32),
            pltpu.VMEM((10, 16, NZ), f32),
            pltpu.SemaphoreType.DMA((COPIES,)),
            pltpu.SemaphoreType.DMA((COPIES,)),
            pltpu.SemaphoreType.DMA((13,)),
            pltpu.SemaphoreType.DMA,
        ],
        compiler_params=pltpu.CompilerParams(
            collective_id=0, has_side_effects=True, vmem_limit_bytes=64 * 2**20
        ),
    )(
        angle_index,
        density.reshape(NY, NZ),
        fixed_mask.reshape(NY, NZ),
        load_mask.reshape(NY, NZ),
        load_fields.reshape(FIELDS, NY, NZ),
    )
    anywhere = pl.BlockSpec(memory_space=pl.ANY)
    x, filtered = pl.pallas_call(
        hand_on,
        out_shape=(
            jax.ShapeDtypeStruct((LOADS, NY, NZ), f32),
            jax.ShapeDtypeStruct((NY, NZ), f32),
        ),
        in_specs=[anywhere] * 2,
        out_specs=(anywhere, anywhere),
        scratch_shapes=[
            pltpu.VMEM((LOADS, NY, NZ), f32),
            pltpu.VMEM((NY, NZ), f32),
            pltpu.SemaphoreType.DMA((LOADS + 1,)),
            pltpu.SemaphoreType.DMA((LOADS + 1,)),
        ],
        compiler_params=pltpu.CompilerParams(vmem_limit_bytes=64 * 2**20),
    )(x, filtered)
    return x.reshape(1, LOADS, 1, NY, NZ), filtered.reshape(1, NY, NZ)


def solution(mesh):
    in_specs = (
        P("space", None, None),
        P("space", None, None),
        P("space", None, None),
        P(None, None, "space", None, None),
        P("sample"),
    )
    out_specs = (P("sample", None, "space", None, None), P("space", None, None))
    return jax.shard_map(body, mesh=mesh, in_specs=in_specs, out_specs=out_specs, check_vma=False)
```
